32 devices in a mesh: section: 2 (over y), dp: 16 (over z, x, core).
Axes of the slice: x: 2, y: 2, z: 4, core: 2. Of those that a mesh axis runs over, the one named last changes fastest.
Arguments:
- section_in: bfloat16 [2, 4096, 768], P('section', 'dp'), may hold values from -6 to 6
- segment_ids: int32 [2, 4096], P(None, 'dp'), may hold values from 0 to 3, as said below
- out_cot: float32 [2, 4096, 1024], P('section', 'dp'), may hold values from -6 to 6
- in_proj: float32 [2, 768, 1024], P('section', 'dp'), may hold values from -0.21875 to 0.21875
- attn_in: float32 [2, 1024, 3072], P('section', 'dp'), may hold values from -0.1875 to 0.1875
- attn_out: float32 [2, 1024, 1024], P('section', 'dp'), may hold values from -1 to 1
- ffn_in: float32 [2, 1024, 4096], P('section', 'dp'), may hold values from -0.1875 to 0.1875
- ffn_out: float32 [2, 4096, 1024], P('section', 'dp'), may hold values from -0.09375 to 0.09375
- norm_gain: float32 [2, 3, 1024], P('section', None, 'dp'), may hold values from 0.5 to 1.5
- norm_bias: float32 [2, 3, 1024], P('section', None, 'dp'), may hold values from -1.75 to 1.75
- cross_in: float32 [1024, 3072], P(('section', 'dp')), may hold values from -0.1875 to 0.1875
- cross_out: float32 [1024, 1024], P(('section', 'dp')), may hold values from -1 to 1
- cross_gain: float32 [1024], P(('section', 'dp')), may hold values from 0.5 to 1.5
- cross_bias: float32 [1024], P(('section', 'dp')), may hold values from -1.75 to 1.75
Outputs:
- section_out: float32 [2, 4096, 1024], P('section', 'dp')
- in_grad: float32 [2, 4096, 768], P('section', 'dp')
- in_proj_grad: float32 [2, 768, 1024], P('section', 'dp')
- attn_in_grad: float32 [2, 1024, 3072], P('section', 'dp')
- attn_out_grad: float32 [2, 1024, 1024], P('section', 'dp')
- ffn_in_grad: float32 [2, 1024, 4096], P('section', 'dp')
- ffn_out_grad: float32 [2, 4096, 1024], P('section', 'dp')
- gain_grad: float32 [2, 3, 1024], P('section', None, 'dp')
- bias_grad: float32 [2, 3, 1024], P('section', None, 'dp')
- cross_in_grad: float32 [1024, 3072], P(('section', 'dp'))
- cross_out_grad: float32 [1024, 1024], P(('section', 'dp'))
- cross_gain_grad: float32 [1024], P(('section', 'dp'))
- cross_bias_grad: float32 [1024], P(('section', 'dp'))
The draws below stay inside these ranges and needn't reach their ends.
Inputs may be any that keep to these rules, and one draw needn't show every extreme that they name: `segment_ids`: within each row and each sequence of 128 tokens the ids never fall, start at 0 and take every value up to 3.
All inputs are finite; a program needn't handle non-finite values.
Results may differ from the reference program's by a relative error of at most 0.018.
Values may be sent and summed in bfloat16 or wider, within the bound.
No kernel may reach another device: no remote copies, remote signals or barrier semaphores. Data moves between devices by JAX's collectives and lax.ppermute only.
A program may use at most 768 MiB of HBM per device.

```python
import jax
import jax.numpy as jnp
from jax import lax

D = 1024
FF = 4096
HEAD_DIM = 64
DIN = 768
SEQ = 128
DOCS = 4
TOKENS = 4096


def draw_segment_ids(key, part):
    key = jax.random.fold_in(key, 11)
    count = 2 * (TOKENS // SEQ)
    seq_keys = jax.random.split(key, count)
    places = jnp.arange(SEQ).astype(jnp.int32)

    def one_sequence(seq_key):
        order = jax.random.permutation(seq_key, SEQ - 1).astype(jnp.int32) + 1
        cuts = order[:DOCS - 1]
        return jnp.sum((places[:, None] >= cuts[None, :]).astype(jnp.int32), axis=1)
    return jax.vmap(one_sequence)(seq_keys).reshape(2, TOKENS).astype(jnp.int32)


def block_scale(key, shape, cuts, least, largest):
    loudness = 1.0
    for position, blocks in cuts:
        heights = jax.random.uniform(jax.random.fold_in(jax.random.fold_in(key, 6), position), (blocks,), jnp.float32, least / len(cuts), largest / len(cuts))
        loudness = loudness * jnp.repeat(jnp.exp(heights), shape[position] // blocks).reshape((-1,) + (1,) * (len(shape) - 1 - position))
    return loudness


def gaussian(own_key, extent, deviation, bound, cuts=(), kind=jnp.bfloat16):
    array = deviation * jax.random.normal(own_key, extent, jnp.float32)
    if cuts:
        array = array * block_scale(own_key, extent, cuts, -0.22, 0.18)
    return jnp.clip(array, -bound, bound).astype(kind)


def setup_inputs(seed: int = 0) -> dict:
    splits = jax.random.split(jax.random.key(seed), 15)
    return {
        "section_in": gaussian(splits[0], (2, TOKENS, DIN), 1.0, 6.0, ((0, 2), (1, 16))),
        "segment_ids": draw_segment_ids(jax.random.fold_in(splits[14], 71), 0),
        "out_cot": gaussian(splits[2], (2, TOKENS, D), 1.0, 6.0, ((0, 2), (1, 16)), jnp.float32),
        "in_proj": gaussian(splits[3], (2, DIN, D), DIN ** -0.5, 0.21875, ((0, 2), (1, 16)), jnp.float32),
        "attn_in": gaussian(splits[4], (2, D, 3 * D), D ** -0.5, 0.1875, ((0, 2), (1, 16)), jnp.float32),
        "attn_out": gaussian(splits[5], (2, D, D), (D * DOCS // SEQ) ** -0.5, 1.0, ((0, 2), (1, 16)), jnp.float32),
        "ffn_in": gaussian(splits[6], (2, D, FF), D ** -0.5, 0.1875, ((0, 2), (1, 16)), jnp.float32),
        "ffn_out": gaussian(splits[7], (2, FF, D), FF ** -0.5, 0.09375, ((0, 2), (1, 16)), jnp.float32),
        "norm_gain": jnp.clip(1.0 + 0.1 * jax.random.normal(splits[8], (2, 3, D), jnp.float32), 0.5, 1.5),
        "norm_bias": gaussian(splits[9], (2, 3, D), 0.3, 1.75, ((0, 2), (2, 16)), jnp.float32),
        "cross_in": gaussian(splits[10], (D, 3 * D), D ** -0.5, 0.1875, ((0, 32),), jnp.float32),
        "cross_out": gaussian(splits[11], (D, D), (D * DOCS // SEQ) ** -0.5, 1.0, ((0, 32),), jnp.float32),
        "cross_gain": jnp.clip(1.0 + 0.1 * jax.random.normal(splits[12], (D,), jnp.float32), 0.5, 1.5),
        "cross_bias": gaussian(splits[13], (D,), 0.3, 1.75, ((0, 32),), jnp.float32),
    }


@jax.custom_vjp
def low(v):
    return lax.optimization_barrier(v.astype(jnp.bfloat16)).astype(jnp.float32)

@jax.custom_vjp
def low_back(v):
    return v

def low_keep(v):
    return (low(v), None)

def low_pass(kept, grad):
    return (grad,)

def back_keep(v):
    return (v, None)

def back_low(kept, grad):
    return (low(grad),)
low.defvjp(low_keep, low_pass)
low_back.defvjp(back_keep, back_low)

def product(left_side, right_side):
    return jnp.dot(left_side, right_side, precision=lax.Precision.HIGHEST, preferred_element_type=jnp.float32)

def layer_norm(values, gain_row, bias_row):
    centre = values - lax.optimization_barrier(jnp.mean(values, axis=-1, keepdims=True))
    spread = lax.optimization_barrier(jnp.mean(centre * centre, axis=-1, keepdims=True))
    return centre * lax.rsqrt(spread + 1e-05) * gain_row + bias_row

def split_heads(values):
    return values.reshape(values.shape[0], values.shape[1] // HEAD_DIM, HEAD_DIM)

def attention(queries, key_rows, value_rows, allowed):
    factor = HEAD_DIM ** (-0.5)
    scores = low_back(jnp.einsum('qhd,khd->hqk', split_heads(queries), split_heads(key_rows), precision=lax.Precision.HIGHEST))
    logits = jnp.where(allowed[None], scores * factor, -1000000000.0)
    exponent = jnp.exp(logits - lax.optimization_barrier(jnp.max(logits, axis=-1, keepdims=True)))
    attn_probs = exponent / lax.optimization_barrier(jnp.sum(exponent, axis=-1, keepdims=True))
    blended = jnp.einsum('hqk,khd->qhd', low(attn_probs), split_heads(value_rows), precision=lax.Precision.HIGHEST)
    return low(low_back(blended.reshape(queries.shape)))

def section_layer(tokens_in, own_rows, memory, mem_rows, weights, cross, decoder):
    w_in, w_qkv, w_attn, w_up, w_down, gain_rows, bias_rows = weights
    width = w_attn.shape[0]
    embedded = low_back(product(tokens_in, w_in))
    first = layer_norm(embedded, gain_rows[0], bias_rows[0])
    packed = low(low_back(product(low(first), w_qkv)))
    allowed = own_rows[:, None] == own_rows[None, :]
    if decoder:
        places = jnp.arange(tokens_in.shape[0]).astype(jnp.int32)
        allowed = allowed & (places[None, :] <= places[:, None])
    blended = attention(packed[:, :width], packed[:, width:2 * width], packed[:, 2 * width:], allowed)
    second = layer_norm(first + low_back(product(blended, w_attn)), gain_rows[1], bias_rows[1])
    if decoder:
        wc_in, wc_out, cross_gain, cross_bias = cross
        cross_q = low(low_back(product(low(second), wc_in[:, :width])))
        cross_kv = low(low_back(product(memory, wc_in[:, width:])))
        cross_mask = own_rows[:, None] == mem_rows[None, :]
        cross_mix = attention(cross_q, cross_kv[:, :width], cross_kv[:, width:], cross_mask)
        third = layer_norm(second + low_back(product(cross_mix, wc_out)), cross_gain, cross_bias)
    else:
        third = second
    inner = low_back(product(low(third), w_up))
    active = low(jax.nn.gelu(inner, approximate=False))
    return layer_norm(third + low_back(product(active, w_down)), gain_rows[2], bias_rows[2])

def forward(segment_ids, section_in, in_proj, attn_in, attn_out, ffn_in, ffn_out, norm_gain, norm_bias, cross_in, cross_out, cross_gain, cross_bias):
    lowered = [low(item) for item in (in_proj, attn_in, attn_out, ffn_in, ffn_out, norm_gain, norm_bias, cross_in, cross_out, cross_gain, cross_bias)]
    encoder_w = tuple((item[0] for item in lowered[:7]))
    decoder_w = tuple((item[1] for item in lowered[:7]))
    cross_w = tuple(lowered[7:])
    count = TOKENS // SEQ
    enc_inputs = section_in[0].reshape(count, SEQ, DIN)
    dec_inputs = section_in[1].reshape(count, SEQ, DIN)
    seg_blocks = segment_ids.reshape(2, count, SEQ)

    def one_sequence(block):
        enc_in, dec_in, enc_seg, dec_seg = block
        encoded = section_layer(enc_in, enc_seg, None, None, encoder_w, cross_w, False)
        memory = low(low_back(encoded))
        decoded = section_layer(dec_in, dec_seg, memory, enc_seg, decoder_w, cross_w, True)
        return (encoded, decoded)
    encoded, decoded = lax.map(jax.checkpoint(one_sequence), (enc_inputs, dec_inputs, seg_blocks[0], seg_blocks[1]))
    return (encoded.reshape(TOKENS, D), decoded.reshape(TOKENS, D))

def reference(section_in, segment_ids, out_cot, in_proj, attn_in, attn_out, ffn_in, ffn_out, norm_gain, norm_bias, cross_in, cross_out, cross_gain, cross_bias):
    floats = (section_in.astype(jnp.float32), in_proj, attn_in, attn_out, ffn_in, ffn_out, norm_gain, norm_bias, cross_in, cross_out, cross_gain, cross_bias)

    def wrapped(*items):
        return forward(segment_ids, *items)
    outputs, pull = jax.vjp(wrapped, *floats)
    grads = pull((out_cot[0], out_cot[1]))
    return (jnp.stack(outputs), grads[0], grads[1], grads[2], grads[3], grads[4], grads[5], grads[6], grads[7], grads[8], grads[9], grads[10], grads[11])
```

```python
import math

import jax
import jax.numpy as jnp
from jax import lax
from jax.sharding import PartitionSpec as P

HEAD_DIM = 64
SEQ = 128
NEG_FILL = -1000000000.0
BF = jnp.bfloat16
F32 = jnp.float32


def swap_core(x):
    n = lax.axis_size("dp")
    return lax.ppermute(x, "dp", [(i, i ^ 1) for i in range(n)])


def swap_pair(x):
    n = lax.axis_size("dp")
    return lax.ppermute(x, "dp", [(i, i ^ 2) for i in range(n)])


def shift_outer(x):
    n = lax.axis_size("dp")
    return lax.ppermute(x, "dp", [(i, (i + 4) % n) for i in range(n)])


def to_decoder(x):
    return lax.ppermute(x, "section", [(0, 1)])


def to_encoder(x):
    return lax.ppermute(x, "section", [(1, 0)])


def gather(x):
    return lax.all_gather(x, "dp", axis=0, tiled=False)


def relative_blocks(me, n):
    m = n // 4
    blk = jnp.arange(n)
    crel = 1 - blk // (2 * m)
    xrel = 1 - (blk % (2 * m)) // m
    zpos = blk % m
    z = (me // 4 - 1 - zpos) % m
    return z * 4 + ((me // 2) % 2 ^ xrel) * 2 + (me % 2 ^ crel)


def order_matrix(order, block, halves=1):
    n = order.shape[0]
    base = order.reshape(2, 1, n // 2, 1) * block
    src = (
        base
        + jnp.arange(halves).reshape(1, halves, 1, 1) * (n * block)
        + jnp.arange(block).reshape(1, 1, 1, block)
    ).reshape(-1)
    return (jnp.arange(src.shape[0])[:, None] == src[None, :]).astype(BF)


def reordered(a, matrix):
    return jnp.dot(a, matrix, preferred_element_type=F32).astype(BF)


def add_low(a, b):
    return (a.astype(F32) + b.astype(F32)).astype(BF)


def reduce_core(part):
    half = part.shape[0] // 2
    return add_low(part[half:], swap_core(part[:half]))


def reduce_rest(part):
    m = lax.axis_size("dp") // 4
    half = part.shape[0] // 2
    part = add_low(part[half:], swap_pair(part[:half]))
    rows = part.shape[0] // m
    total = part[:rows]
    for k in range(1, m):
        total = shift_outer(total.astype(BF)).astype(F32) + part[k * rows : (k + 1) * rows].astype(
            F32
        )
    return total


def reduce_rel(part):
    return reduce_rest(reduce_core(part))


def mm(a, w):
    return jnp.dot(a, w, preferred_element_type=F32)


def outer_low(a, dy):
    return jnp.einsum("ti,to->io", a, dy, preferred_element_type=F32).astype(BF)


def mm_t(dy, w):
    return jnp.einsum("to,io->ti", dy, w, preferred_element_type=F32)


def norm_forward(values, gain_row, bias_row):
    centre = values - jnp.mean(values, axis=-1, keepdims=True)
    inverse = lax.rsqrt(jnp.mean(centre * centre, axis=-1, keepdims=True) + 1e-05)
    normed = centre * inverse
    return (normed * gain_row + bias_row, normed, inverse)


def norm_backward(upstream, normed, inverse, gain_row):
    scaled = upstream * gain_row
    grad_in = inverse * (
        scaled
        - jnp.mean(scaled, axis=-1, keepdims=True)
        - normed * jnp.mean(scaled * normed, axis=-1, keepdims=True)
    )
    return (grad_in, jnp.sum(upstream * normed, axis=0), jnp.sum(upstream, axis=0))


def heads(values):
    return values.reshape(-1, SEQ, values.shape[1] // HEAD_DIM, HEAD_DIM)


def attend(queries, key_rows, value_rows, allowed):
    factor = HEAD_DIM ** (-0.5)
    scores = jnp.einsum(
        "bqhd,bkhd->bhqk", heads(queries), heads(key_rows), preferred_element_type=F32
    )
    logits = jnp.where(allowed[:, None], scores * factor, NEG_FILL)
    exponent = jnp.exp(logits - jnp.max(logits, axis=-1, keepdims=True))
    probs = exponent / jnp.sum(exponent, axis=-1, keepdims=True)
    blended = jnp.einsum(
        "bhqk,bkhd->bqhd", probs.astype(BF), heads(value_rows), preferred_element_type=F32
    )
    return (blended.reshape(queries.shape).astype(BF), probs)


def attend_back(grad_blended, queries, key_rows, value_rows, probs):
    factor = HEAD_DIM ** (-0.5)
    grad_heads = heads(grad_blended)
    grad_probs = jnp.einsum(
        "bqhd,bkhd->bhqk", grad_heads, heads(value_rows), preferred_element_type=F32
    )
    grad_values = jnp.einsum(
        "bhqk,bqhd->bkhd", probs.astype(BF), grad_heads, preferred_element_type=F32
    )
    centred = jnp.sum(probs * grad_probs, axis=-1, keepdims=True)
    grad_scores = (probs * (grad_probs - centred) * factor).astype(BF)
    grad_queries = jnp.einsum(
        "bhqk,bkhd->bqhd", grad_scores, heads(key_rows), preferred_element_type=F32
    )
    grad_keys = jnp.einsum(
        "bhqk,bqhd->bkhd", grad_scores, heads(queries), preferred_element_type=F32
    )
    shape = queries.shape
    return (
        grad_queries.reshape(shape).astype(BF),
        grad_keys.reshape(shape).astype(BF),
        grad_values.reshape(shape).astype(BF),
    )


def ffn_forward(third, w_up, w_down, gain_row, bias_row):
    third_low = third.astype(BF)
    inner = mm(third_low, w_up)
    erf = lax.erf(inner * (1.0 / math.sqrt(2.0)))
    active = (0.5 * inner * (1.0 + erf)).astype(BF)
    slope = (
        0.5 * (1.0 + erf) + inner * jnp.exp(-0.5 * inner * inner) * (1.0 / math.sqrt(2.0 * math.pi))
    ).astype(BF)
    out, normed, inverse = norm_forward(third + mm(active, w_down), gain_row, bias_row)
    return (out, third_low, active, slope, normed, inverse)


def ffn_backward(cot, normed, inverse, gain_row, slope, w_up, w_down):
    grad, dg, db = norm_backward(cot, normed, inverse, gain_row)
    branch = grad.astype(BF)
    d_inner = (mm_t(branch, w_down) * slope.astype(F32)).astype(BF)
    return (grad + mm_t(d_inner, w_up), branch, d_inner, dg, db)


def shards(
    section_in,
    segment_ids,
    out_cot,
    in_proj,
    attn_in,
    attn_out,
    ffn_in,
    ffn_out,
    norm_gain,
    norm_bias,
    cross_in,
    cross_out,
    cross_gain,
    cross_bias,
):
    n = lax.axis_size("dp")
    me = lax.axis_index("dp")
    core = me % 2
    is_dec = lax.axis_index("section") == 1
    width = attn_out.shape[2]
    inner_width = ffn_in.shape[2]
    d_loc = attn_out.shape[1]
    in_loc = in_proj.shape[1]
    c_loc = cross_in.shape[0]
    in_width = in_loc * n

    params = jnp.concatenate(
        [norm_gain[0].reshape(-1), norm_bias[0].reshape(-1), cross_gain, cross_bias]
    ).astype(BF)
    n_par = params.shape[0]
    tail = jnp.pad(params[None], ((0, d_loc - in_loc - 1), (0, width - n_par)))
    pack1 = jnp.concatenate(
        [
            attn_in[0].astype(BF),
            attn_out[0].astype(BF),
            jnp.concatenate([in_proj[0].astype(BF), tail], axis=0),
        ],
        axis=1,
    )
    q4 = inner_width // width
    pack2 = jnp.concatenate(
        [
            ffn_in[0].astype(BF),
            ffn_out[0].astype(BF).reshape(q4, d_loc, width).transpose(1, 0, 2).reshape(d_loc, -1),
            jnp.concatenate([cross_in, cross_out], axis=1).astype(BF),
        ],
        axis=0,
    )
    all1 = gather(pack1)
    all2 = gather(pack2)

    w_qkv = all1[:, :, : 3 * width].reshape(width, 3 * width)
    w_attn = all1[:, :, 3 * width : 4 * width].reshape(width, width)
    last = all1[:, :, 4 * width :]
    w_in = last[:, :in_loc].reshape(in_width, width)
    pars = last[:, in_loc, :n_par].astype(F32)
    gains = pars[:, : 3 * d_loc].reshape(n, 3, d_loc).transpose(1, 0, 2).reshape(3, width)
    biases = (
        pars[:, 3 * d_loc : 6 * d_loc].reshape(n, 3, d_loc).transpose(1, 0, 2).reshape(3, width)
    )
    w_up = all2[:, :d_loc].reshape(width, inner_width)
    w_down = (
        all2[:, d_loc : 2 * d_loc]
        .reshape(n, d_loc, q4, width)
        .transpose(0, 2, 1, 3)
        .reshape(inner_width, width)
    )
    own_cross = all2[:, 2 * d_loc :].reshape(n * c_loc, 4 * width)
    half = n * c_loc // 2
    mine = to_decoder(lax.dynamic_slice_in_dim(own_cross, core * half, half, 0))
    other = swap_core(mine)
    w_cross = jnp.concatenate(
        [jnp.where(core == 0, mine, other), jnp.where(core == 0, other, mine), own_cross], axis=0
    )
    w_cin, w_cout = w_cross[:, : 3 * width], w_cross[:, 3 * width :]
    own_cpar = pars[:, 6 * d_loc :].astype(BF)
    cpar = jnp.stack([to_decoder(own_cpar), own_cpar]).astype(F32)
    c_gain = cpar[:, :, :c_loc].reshape(width)
    c_bias = cpar[:, :, c_loc:].reshape(width)

    order = relative_blocks(me, n)
    perm_d = order_matrix(order, d_loc)
    perm_in = order_matrix(order, in_loc)
    perm_cross = order_matrix(order, c_loc, 2)

    tokens = section_in[0]
    cot = out_cot[0]
    seqs = tokens.shape[0] // SEQ
    seg = segment_ids.reshape(2, seqs, SEQ)
    own_seg = jnp.where(is_dec, seg[1], seg[0])
    enc_seg = seg[0]
    places = jnp.arange(SEQ)
    causal = (places[None, :] <= places[:, None]) | jnp.logical_not(is_dec)
    self_mask = (own_seg[:, :, None] == own_seg[:, None, :]) & causal[None]
    cross_mask = own_seg[:, :, None] == enc_seg[:, None, :]

    first, xa, ia = norm_forward(mm(tokens, w_in), gains[0], biases[0])
    first_low = first.astype(BF)
    packed = mm(first_low, w_qkv).astype(BF)
    pq, pk, pv = packed[:, :width], packed[:, width : 2 * width], packed[:, 2 * width :]
    blended, probs_self = attend(pq, pk, pv, self_mask)
    second, xb, ib = norm_forward(first + mm(blended, w_attn), gains[1], biases[1])
    second_low = second.astype(BF)

    encoded = ffn_forward(second, w_up, w_down, gains[2], biases[2])[0]
    memory = to_decoder(encoded.astype(BF))

    cross_q = mm(second_low, w_cin[:, :width]).astype(BF)
    cross_kv = mm(memory, w_cin[:, width:]).astype(BF)
    ck, cv = cross_kv[:, :width], cross_kv[:, width:]
    cross_mix, probs_cross = attend(cross_q, ck, cv, cross_mask)
    third_c, xc, ic = norm_forward(second + mm(cross_mix, w_cout), c_gain, c_bias)
    third = jnp.where(is_dec, third_c, second)

    output, third_low, active, slope, xd, idd = ffn_forward(
        third, w_up, w_down, gains[2], biases[2]
    )

    grad_third = ffn_backward(cot, xd, idd, gains[2], slope, w_up, w_down)[0]
    grad_resid, dg_c, db_c = norm_backward(grad_third, xc, ic, c_gain)
    d_cbranch = grad_resid.astype(BF)
    d_cmix = mm_t(d_cbranch, w_cout).astype(BF)
    d_cq, d_ck, d_cv = attend_back(d_cmix, cross_q, ck, cv, probs_cross)
    d_ckv = jnp.concatenate([d_ck, d_cv], axis=1)
    grad_memory = to_encoder(mm_t(d_ckv, w_cin[:, width:]).astype(BF))
    grad_second_dec = grad_resid + mm_t(d_cq, w_cin[:, :width])

    cross_part = jnp.concatenate(
        [
            outer_low(reordered(second_low, perm_cross), d_cq),
            outer_low(reordered(memory, perm_cross), d_ckv),
            outer_low(reordered(cross_mix, perm_cross), d_cbranch),
        ],
        axis=1,
    )
    cross_part = reduce_core(cross_part)
    mid = cross_part.shape[0] // 2
    cross_part = jnp.where(is_dec, cross_part[mid:], to_encoder(cross_part[:mid]))
    cross_total = reduce_rest(cross_part)
    cvec = jnp.stack([dg_c, db_c]).astype(BF).reshape(2, 2, n, c_loc)
    cvec = jnp.where(is_dec, cvec[:, 1], to_encoder(cvec[:, 0])).transpose(1, 0, 2)

    grad_third, branch_d, d_inner, dg_d, db_d = ffn_backward(
        cot + grad_memory.astype(F32), xd, idd, gains[2], slope, w_up, w_down
    )
    blk = inner_width // n
    active_rel = jnp.concatenate(
        [lax.dynamic_slice_in_dim(active, order[k] * blk, blk, 1) for k in range(n)], axis=1
    )
    down_total = reduce_rel(outer_low(active_rel, branch_d))
    up_total = reduce_rel(outer_low(reordered(third_low, perm_d), d_inner))
    grad_second = jnp.where(is_dec, grad_second_dec, grad_third)

    grad_b, dg_b, db_b = norm_backward(grad_second, xb, ib, gains[1])
    branch_b = grad_b.astype(BF)
    attn_total = reduce_rel(outer_low(reordered(blended, perm_d), branch_b))
    d_blended = mm_t(branch_b, w_attn).astype(BF)
    d_q, d_k, d_v = attend_back(d_blended, pq, pk, pv, probs_self)
    d_packed = jnp.concatenate([d_q, d_k, d_v], axis=1)
    qkv_total = reduce_rel(outer_low(reordered(first_low, perm_d), d_packed))
    grad_first = grad_b + mm_t(d_packed, w_qkv)
    grad_embed, dg_a, db_a = norm_backward(grad_first, xa, ia, gains[0])
    d_embed = grad_embed.astype(BF)
    in_grad = mm_t(d_embed, w_in)
    in_part = outer_low(reordered(tokens, perm_in), d_embed).reshape(n, in_loc, width)
    vecs = jnp.stack([dg_a, dg_b, dg_d, db_a, db_b, db_d]).astype(BF)
    vecs = vecs.reshape(6, n, d_loc).transpose(1, 0, 2).reshape(n, 6 * d_loc)
    vecs = jnp.concatenate([vecs, cvec.reshape(n, 2 * c_loc)], axis=1)[order]
    vecs = jnp.pad(vecs[:, None, :], ((0, 0), (0, d_loc - in_loc - 1), (0, width - n_par)))
    in_part = jnp.concatenate([in_part, vecs], axis=1).reshape(n * d_loc, width)
    in_total = reduce_rel(in_part)
    row = in_total[in_loc]
    gain_total = row[: 3 * d_loc].reshape(1, 3, d_loc)
    bias_total = row[3 * d_loc : 6 * d_loc].reshape(1, 3, d_loc)

    return (
        output[None],
        in_grad[None],
        in_total[:in_loc][None],
        qkv_total[None],
        attn_total[None],
        up_total[None],
        down_total[None],
        gain_total,
        bias_total,
        cross_total[:, : 3 * width],
        cross_total[:, 3 * width :],
        row[6 * d_loc : 6 * d_loc + c_loc],
        row[6 * d_loc + c_loc : n_par],
    )


def solution(mesh):
    placed = (
        P("section", "dp", None),
        P(None, "dp"),
        P("section", "dp", None),
        P("section", "dp", None),
        P("section", "dp", None),
        P("section", "dp", None),
        P("section", "dp", None),
        P("section", "dp", None),
        P("section", None, "dp"),
        P("section", None, "dp"),
        P(("section", "dp"), None),
        P(("section", "dp"), None),
        P(("section", "dp")),
        P(("section", "dp")),
    )
    return jax.shard_map(
        shards,
        mesh=mesh,
        in_specs=placed,
        out_specs=(
            P("section", "dp", None),
            P("section", "dp", None),
            P("section", "dp", None),
            P("section", "dp", None),
            P("section", "dp", None),
            P("section", "dp", None),
            P("section", "dp", None),
            P("section", None, "dp"),
            P("section", None, "dp"),
            P(("section", "dp"), None),
            P(("section", "dp"), None),
            P(("section", "dp")),
            P(("section", "dp")),
        ),
        check_vma=False,
    )
```

```python
import math

import jax
import jax.numpy as jnp
from jax import lax
from jax.experimental import pallas as pl
from jax.experimental.pallas import tpu as pltpu
from jax.sharding import PartitionSpec as P

HEAD_DIM = 64
SEQ = 128
NEG_FILL = -1000000000.0
BF = jnp.bfloat16
F32 = jnp.float32


def swap_core(x):
    n = lax.axis_size("dp")
    return lax.ppermute(x, "dp", [(i, i ^ 1) for i in range(n)])


def swap_pair(x):
    n = lax.axis_size("dp")
    return lax.ppermute(x, "dp", [(i, i ^ 2) for i in range(n)])


def spread_outer(x):
    n = lax.axis_size("dp")
    groups = [list(range(at, n, 4)) for at in range(4)]
    x = x.reshape(n // 4, -1, x.shape[1])
    return lax.all_to_all(x, "dp", 0, 0, axis_index_groups=groups)


def to_decoder(x):
    return lax.ppermute(x, "section", [(0, 1)])


def to_encoder(x):
    return lax.ppermute(x, "section", [(1, 0)])


def after(x, *deps):
    return lax.optimization_barrier((x,) + deps)[0]


def relative_blocks(me, n):
    m = n // 4
    blk = jnp.arange(n)
    crel = 1 - blk // (2 * m)
    xrel = 1 - (blk % (2 * m)) // m
    return (blk % m) * 4 + ((me // 2) % 2 ^ xrel) * 2 + (me % 2 ^ crel)


def order_matrix(order, block, halves=1):
    n = order.shape[0]
    base = order.reshape(2, 1, n // 2, 1) * block
    src = (
        base
        + jnp.arange(halves).reshape(1, halves, 1, 1) * (n * block)
        + jnp.arange(block).reshape(1, 1, 1, block)
    ).reshape(-1)
    return (jnp.arange(src.shape[0])[:, None] == src[None, :]).astype(BF)


def reordered(a, matrix):
    return jnp.einsum("tk,kr->rt", a, matrix, preferred_element_type=F32).astype(BF)


class Chain:
    def __init__(self):
        self.last = ()

    def __call__(self, x):
        return after(x, *self.last) if self.last else x

    def mark(self, *outs):
        self.last = outs
        return outs[0]


def add_low(a, b):
    return (a.astype(F32) + b.astype(F32)).astype(BF)


def summed(blocks):
    return jnp.sum(blocks.astype(F32), axis=0)


class Part:
    def __init__(self, chain, a, dy, got=None, picks=(), columns=None):
        self.chain, self.a, self.dy, self.picks, self.columns = chain, a, dy, picks, columns
        self.k = a.shape[-2]
        self.got = got or [swap_core(piece) for piece in self.outer(0, self.k // 2, pieces=True)]

    def outer(self, first, count, *adds, pieces=False):
        dy = self.chain(self.dy)
        kinds = {"picks": self.picks, "pieces": pieces, "columns": self.columns}
        made = outer(self.a, first, count, dy, *adds, **kinds)
        self.chain.mark(*(made if pieces else (made,)))
        return made

    def pair(self, *deps):
        q, mid = self.k // 4, len(self.got) // 2
        half = self.outer(2 * q, q, (self.got[:mid], 0))
        self.pair_got = swap_pair(after(half, *deps) if deps else half)

    def add(self):
        q, mid = self.k // 4, len(self.got) // 2
        self.mine = self.outer(3 * q, q, (self.got[mid:], 0), ((self.pair_got,), 0))

    def spread(self, *deps):
        self.blocks = spread_outer(after(self.mine, *deps) if deps else self.mine)

    def total(self):
        return summed(self.blocks)


VMEM_LIMIT = 58 * 2**20


def dot(a, b):
    return jnp.dot(a, b, preferred_element_type=F32)


def dot_nt(a, b):
    return lax.dot_general(a, b, (((1,), (1,)), ((), ())), preferred_element_type=F32)


def dot_tn(a, b):
    return lax.dot_general(a, b, (((0,), (0,)), ((), ())), preferred_element_type=F32)


SMEM_SPEC = pl.BlockSpec(memory_space=pltpu.SMEM)
VMEM_SPEC = pl.BlockSpec(memory_space=pltpu.VMEM)
ANY_SPEC = pl.BlockSpec(memory_space=pl.ANY)


def shape_of(rows, columns, dtype=F32):
    return jax.ShapeDtypeStruct((rows, columns), dtype)


def kernel_call(body, out_shape, args, specs, out_specs, name, scratch=(), cost=0):
    return pl.pallas_call(
        body,
        in_specs=specs,
        out_specs=out_specs,
        out_shape=out_shape,
        scratch_shapes=scratch,
        compiler_params=pltpu.CompilerParams(vmem_limit_bytes=VMEM_LIMIT),
        cost_estimate=pl.CostEstimate(flops=cost, bytes_accessed=0, transcendentals=0),
        name=name,
    )(*args)


class Rows:
    def __init__(self, d_loc, inner_width, width):
        self.d = d_loc
        self.width = width
        self.ups = inner_width // width
        self.down_rows = self.ups * d_loc
        self.w_in = 0
        self.qkv = d_loc
        self.attn = 4 * d_loc
        self.up = 5 * d_loc
        self.down = self.up + self.ups * d_loc


def fetch(src, row, rows, dst, sem):
    copy = pltpu.make_async_copy(src.at[:, pl.ds(row, rows)], dst, sem)
    copy.start()
    return copy


def whole(ref):
    value = ref[...]
    return value.reshape(value.shape[0] * value.shape[1], value.shape[2])


def halves(x):
    low_half = lax.broadcasted_iota(jnp.int32, x.shape, 1) < HEAD_DIM
    zero = jnp.zeros_like(x)
    return jnp.where(low_half, x, zero), jnp.where(low_half, zero, x)


def joined(a, b):
    return jnp.where(lax.broadcasted_iota(jnp.int32, a.shape, 1) < HEAD_DIM, a, b)


def softmax_t(scores, mask):
    logits = jnp.where(mask, scores, NEG_FILL)
    e = jnp.exp(logits - jnp.max(logits, axis=0, keepdims=True))
    return e * (1.0 / jnp.sum(e, axis=0, keepdims=True))


FACTOR = HEAD_DIM ** (-0.5)


def attend_lanes(q, k, v, mask):
    scaled = q * jnp.asarray(FACTOR, BF)
    scores = [dot_nt(k, part) for part in halves(scaled)]
    probs = [softmax_t(s, mask).astype(BF) for s in scores]
    return joined(*[dot_tn(p, v) for p in probs]).astype(BF)


def attend_back_lanes(g, q, k, v, mask):
    scaled = q * jnp.asarray(FACTOR, BF)
    grads = []
    for q_part, g_part in zip(halves(scaled), halves(g)):
        probs = softmax_t(dot_nt(k, q_part), mask)
        d_probs = dot_nt(v, g_part)
        centred = jnp.sum(probs * d_probs, axis=0, keepdims=True)
        d_s = (probs * (d_probs - centred) * FACTOR).astype(BF)
        grads.append((dot_tn(d_s, k), dot(d_s, q), dot(probs.astype(BF), g)))
    return [joined(a, b).astype(BF) for a, b in zip(*grads)]


def lanes_of(i, offset=0):
    return pl.ds(pl.multiple_of(offset + i * 128, 128), 128)


def attend_all(q_ref, q_at, kv_ref, k_at, v_at, mask_ref, out_ref, width):
    rows = q_ref.shape[0]

    def step(i, carry):
        for b in range(rows // SEQ):
            s = pl.ds(b * SEQ, SEQ)
            out_ref[s, lanes_of(i)] = attend_lanes(
                q_ref[s, lanes_of(i, q_at)],
                kv_ref[s, lanes_of(i, k_at)],
                kv_ref[s, lanes_of(i, v_at)],
                mask_ref[b] > 0,
            )
        return carry

    lax.fori_loop(0, width // 128, step, 0)


def attend_back_all(g_ref, q_ref, q_at, kv_ref, k_at, v_at, mask_ref, out_ref, width):
    rows = g_ref.shape[0]

    def step(i, carry):
        for b in range(rows // SEQ):
            s = pl.ds(b * SEQ, SEQ)
            parts = attend_back_lanes(
                g_ref[s, lanes_of(i)],
                q_ref[s, lanes_of(i, q_at)],
                kv_ref[s, lanes_of(i, k_at)],
                kv_ref[s, lanes_of(i, v_at)],
                mask_ref[b] > 0,
            )
            for at, part in enumerate(parts):
                out_ref[s, lanes_of(i, at * width)] = part
        return carry

    lax.fori_loop(0, width // 128, step, 0)


def norm_values(values, gain, bias):
    centre = values - jnp.mean(values, axis=-1, keepdims=True)
    inverse = lax.rsqrt(jnp.mean(centre * centre, axis=-1, keepdims=True) + 1e-05)
    normed = centre * inverse
    return normed * gain + bias, normed, inverse


def norm_back_values(upstream, normed, inverse, gain):
    scaled = upstream * gain
    return inverse * (
        scaled
        - jnp.mean(scaled, axis=-1, keepdims=True)
        - normed * jnp.mean(scaled * normed, axis=-1, keepdims=True)
    )


def gelu_parts(inner, with_slope):
    erf = 1.0 + lax.erf(inner * (1.0 / math.sqrt(2.0)))
    active = (0.5 * inner * erf).astype(BF)
    if not with_slope:
        return active
    bell = jnp.exp(-0.5 * inner * inner) * (1.0 / math.sqrt(2.0 * math.pi))
    return active, (0.5 * erf + inner * bell).astype(BF)


BLOCK = 512


def column(j, size=BLOCK):
    return pl.ds(pl.multiple_of(j * size, size), size)


def blocks_loop(count, step):
    lax.fori_loop(0, count, lambda j, carry: (step(j), carry)[1], 0)


def front(tokens, mask, weights, rows_of, gains, biases):
    t = tokens.shape[0]
    n, _, width = weights.shape
    d, ups = rows_of.d, rows_of.ups
    inner_width = ups * width

    def kernel(x_ref, mask_ref, g0, g1, g2, b0, b1, b2, w_hbm, *refs):
        xa_hbm, ia_ref, first_hbm, packed_hbm, mix_hbm, second_hbm, xb_hbm, ib_ref, second_low_hbm, memory_ref = refs[:10]
        w_in, w_qkv, w_attn, w_up, w_down, held, normed, low, packed, mix, second_low, total, active = refs[10:23]
        sems, out_sems = refs[23:]
        first_copy = fetch(w_hbm, rows_of.w_in, d, w_in, sems.at[0])
        qkv_copies = [fetch(w_hbm, rows_of.qkv + i * d, d, w_qkv.at[i], sems.at[1 + i]) for i in range(3)]
        attn_copy = fetch(w_hbm, rows_of.attn, d, w_attn, sems.at[4])
        up_copies = [fetch(w_hbm, rows_of.up + i * d, d, w_up.at[i], sems.at[6 + i]) for i in range(ups)]
        down_copy = fetch(w_hbm, rows_of.down, rows_of.down_rows, w_down, sems.at[5])
        outs = []

        def put(src, dst):
            outs.append(pltpu.make_async_copy(src, dst, out_sems.at[len(outs)]))
            outs[-1].start()

        first_copy.wait()
        first, xa, ia = norm_values(dot(x_ref[...], whole(w_in)), g0[...], b0[...])
        held[...] = first
        normed[...] = xa
        ia_ref[...] = ia
        low[...] = first.astype(BF)
        put(normed, xa_hbm)
        put(low, first_hbm)
        for copy in qkv_copies:
            copy.wait()

        def project(j):
            packed[:, column(j, width)] = dot(
                low[...], w_qkv[j].reshape(n * d, width)
            ).astype(BF)

        blocks_loop(3, project)
        put(packed, packed_hbm)
        attend_all(packed, 0, packed, width, 2 * width, mask_ref, mix, width)
        put(mix, mix_hbm)
        attn_copy.wait()
        second, xb, ib = norm_values(held[...] + dot(mix[...], whole(w_attn)), g1[...], b1[...])
        outs[0].wait()
        held[...] = second
        normed[...] = xb
        ib_ref[...] = ib
        second_low[...] = second.astype(BF)
        put(held, second_hbm)
        put(normed, xb_hbm)
        put(second_low, second_low_hbm)
        for copy in up_copies:
            copy.wait()

        def forward(j):
            active[j] = gelu_parts(dot(second_low[...], w_up[j].reshape(n * d, width)), False)

        blocks_loop(ups, forward)
        down_copy.wait()
        total[...] = second

        def forward_down(j):
            rows = pl.ds(j * (n // ups), n // ups)
            total[...] += dot(active[j], w_down[rows].reshape(width, width))

        blocks_loop(ups, forward_down)
        memory_ref[...] = norm_values(total[...], g2[...], b2[...])[0].astype(BF)
        for copy in outs[1:]:
            copy.wait()

    value, low, vector = shape_of(t, width), shape_of(t, width, BF), shape_of(t, 1)
    big = lambda *shape: pltpu.VMEM(shape, BF)
    return kernel_call(
        kernel,
        (value, vector, low, shape_of(t, 3 * width, BF), low, value, value, vector, low, low),
        (tokens, mask, *gains, *biases, weights),
        [VMEM_SPEC] * 8 + [ANY_SPEC],
        (ANY_SPEC, VMEM_SPEC) + (ANY_SPEC,) * 5 + (VMEM_SPEC, ANY_SPEC, VMEM_SPEC),
        "front",
        scratch=[
            big(n, d, width),
            big(3, n, d, width),
            big(n, d, width),
            big(ups, n, d, width),
            big(n, rows_of.down_rows, width),
            pltpu.VMEM((t, width), F32),
            pltpu.VMEM((t, width), F32),
            big(t, width),
            big(t, 3 * width),
            big(t, width),
            big(t, width),
            pltpu.VMEM((t, width), F32),
            big(ups, t, width),
            pltpu.SemaphoreType.DMA((6 + ups,)),
            pltpu.SemaphoreType.DMA((7,)),
        ],
    )


class Cross:
    def __init__(self, weights):
        self.n, rows, self.width = weights.shape
        self.c = rows // 8
        if self.c % 16:
            both = weights.reshape(self.n, 2, 4, self.c, self.width).transpose(2, 1, 0, 3, 4)
            weights = both.reshape(4, 2 * self.n * self.c, self.width)
        self.weights = weights

    @property
    def scratch(self):
        return pltpu.VMEM((4, 2, self.n, self.c, self.width), BF)

    def start(self, ref, dst, sems, groups):
        copies = {}
        for i in groups:
            copies[i] = []
            for s in range(2):
                if self.c % 16:
                    count = self.n * self.c
                    src = ref.at[i, pl.ds(s * count, count)].reshape(self.n, self.c, self.width)
                else:
                    src = ref.at[:, pl.ds((4 * s + i) * self.c, self.c)]
                copies[i].append(pltpu.make_async_copy(src, dst.at[i, s], sems.at[i, s]))
                copies[i][-1].start()
        return copies

    def matrix(self, ref, i):
        return ref[i].reshape(2 * self.n * self.c, self.width)


def cross_query(low, cross):
    t, width = low.shape

    def kernel(low_ref, w_hbm, out_ref, w, sems):
        for copy in cross.start(w_hbm, w, sems, (0,))[0]:
            copy.wait()
        out_ref[...] = dot(low_ref[...], cross.matrix(w, 0)).astype(BF)

    return kernel_call(
        kernel,
        shape_of(t, width, BF),
        (low, cross.weights),
        [VMEM_SPEC, ANY_SPEC],
        VMEM_SPEC,
        "cross_query",
        scratch=[cross.scratch, pltpu.SemaphoreType.DMA((4, 2))],
    )


def cross_query_back(resid, d_cross, cross):
    t, width = resid.shape

    def kernel(resid_ref, d_ref, w_hbm, out_ref, w, sems):
        for copy in cross.start(w_hbm, w, sems, (0,))[0]:
            copy.wait()
        out_ref[...] = resid_ref[...] + dot_nt(d_ref[:, :width], cross.matrix(w, 0))

    return kernel_call(
        kernel,
        shape_of(t, width),
        (resid, d_cross, cross.weights),
        [VMEM_SPEC, VMEM_SPEC, ANY_SPEC],
        VMEM_SPEC,
        "cross_query_back",
        scratch=[cross.scratch, pltpu.SemaphoreType.DMA((4, 2))],
    )


def decoder_middle(info, memory, cross_q, second, cot, mask, weights, rows_of, cross, c_gain, c_bias, gain, bias):
    t, width = second.shape
    n, d, ups = weights.shape[0], rows_of.d, rows_of.ups
    inner_width = ups * width
    block = inner_width // n
    ordered = block % 128 == 0
    per = n // ups

    def kernel(info_ref, memory_ref, q_ref, mask_ref, cg_ref, cb_ref, g_ref, b_ref, second_hbm, cot_hbm, w_hbm, c_hbm, *refs):
        out_hbm, normed_hbm, inv_ref, third_hbm, active_hbm, slope_hbm = refs[:6]
        mix_ref, d_qkv_ref, d_memory_ref, resid_ref, dg_ref, db_ref = refs[6:12]
        w_c, w_up, w_down, kv, third, low, active, slope, out, normed, c_normed, total, cot = refs[12:25]
        d_branch_ref, cross_sems, sems, act_sems = refs[25:]
        is_dec = info_ref[1] == 1
        copies = cross.start(c_hbm, w_c, cross_sems, (1, 2, 3))
        get_second = pltpu.make_async_copy(second_hbm, third, sems.at[0])
        get_cot = pltpu.make_async_copy(cot_hbm, cot, sems.at[1])
        get_second.start()
        up_copies = [fetch(w_hbm, rows_of.up + i * d, d, w_up.at[i], sems.at[8 + i]) for i in range(ups)]
        down_copy = fetch(w_hbm, rows_of.down, rows_of.down_rows, w_down, sems.at[7])
        get_cot.start()
        for i in (1, 2):
            for copy in copies[i]:
                copy.wait()
            kv[:, (i - 1) * width : i * width] = dot(memory_ref[...], cross.matrix(w_c, i)).astype(BF)
        attend_all(q_ref, 0, kv, 0, width, mask_ref, mix_ref, width)
        get_second.wait()
        for copy in copies[3]:
            copy.wait()
        values = third[...] + dot(mix_ref[...], cross.matrix(w_c, 3))
        third_c, normed_c, inverse_c = norm_values(values, cg_ref[...], cb_ref[...])
        c_normed[...] = normed_c
        third[...] = jnp.where(is_dec, third_c, third[...])
        low[...] = third[...].astype(BF)
        outs = [pltpu.make_async_copy(low, third_hbm, sems.at[2])]
        outs[-1].start()
        for copy in up_copies:
            copy.wait()

        def forward(j):
            active[j], slope[j] = gelu_parts(dot(low[...], w_up[j].reshape(n * d, width)), True)

        blocks_loop(ups, forward)
        if not ordered:
            outs.append(pltpu.make_async_copy(active, active_hbm, act_sems.at[0]))
            outs[-1].start()
        for j in range(n if ordered else 0):
            place = info_ref[2 + j]
            outs.append(
                pltpu.make_async_copy(
                    active.at[j // per, :, pl.ds((j % per) * block, block)],
                    active_hbm.at[:, column(place, block)],
                    act_sems.at[j],
                )
            )
            outs[-1].start()
        outs.append(pltpu.make_async_copy(slope, slope_hbm, sems.at[4]))
        outs[-1].start()
        down_copy.wait()
        total[...] = third[...]

        def forward_down(j):
            total[...] += dot(active[j], w_down[pl.ds(j * per, per)].reshape(width, width))

        blocks_loop(ups, forward_down)
        last, normed_d, inverse_d = norm_values(total[...], g_ref[...], b_ref[...])
        out[...] = last
        normed[...] = normed_d
        inv_ref[...] = inverse_d
        outs += [
            pltpu.make_async_copy(out, out_hbm, sems.at[5]),
            pltpu.make_async_copy(normed, normed_hbm, sems.at[6]),
        ]
        outs[-2].start()
        outs[-1].start()
        get_cot.wait()
        grad = norm_back_values(cot[...], normed_d, inverse_d, g_ref[...])
        total[...] = grad
        d_branch_ref[...] = grad.astype(BF)

        def backward(j):
            d_act = dot_nt(d_branch_ref[...], w_down[pl.ds(j * per, per)].reshape(width, width))
            d_inner = (d_act * slope[j].astype(F32)).astype(BF)
            total[...] += dot_nt(d_inner, w_up[j].reshape(n * d, width))

        blocks_loop(ups, backward)
        grad = total[...]
        dg_ref[...] = jnp.sum(grad * c_normed[...], axis=0, keepdims=True)
        db_ref[...] = jnp.sum(grad, axis=0, keepdims=True)
        resid = norm_back_values(grad, c_normed[...], inverse_c, cg_ref[...])
        resid_ref[...] = resid
        d_branch_ref[...] = resid.astype(BF)
        outs[0].wait()
        low[...] = dot_nt(d_branch_ref[...], cross.matrix(w_c, 3)).astype(BF)
        attend_back_all(low, q_ref, 0, kv, 0, width, mask_ref, d_qkv_ref, width)
        d_qkv_ref[:, 3 * width :] = d_branch_ref[...]
        d_memory = dot_nt(d_qkv_ref[:, width : 2 * width], cross.matrix(w_c, 1))
        d_memory_ref[...] = (
            d_memory + dot_nt(d_qkv_ref[:, 2 * width : 3 * width], cross.matrix(w_c, 2))
        ).astype(BF)
        for copy in outs[1:]:
            copy.wait()

    value, low = shape_of(t, width), shape_of(t, width, BF)
    vector, blocked = shape_of(1, width), jax.ShapeDtypeStruct((ups, t, width), BF)
    big = lambda *shape: pltpu.VMEM(shape, BF)
    return kernel_call(
        kernel,
        (value, value, shape_of(t, 1), low)
        + (shape_of(t, inner_width, BF) if ordered else blocked, blocked)
        + (low, shape_of(t, 4 * width, BF), low, value, vector, vector),
        (info, memory, cross_q, mask, c_gain, c_bias, gain, bias, second, cot, weights, cross.weights),
        [SMEM_SPEC] + [VMEM_SPEC] * 7 + [ANY_SPEC] * 4,
        (ANY_SPEC, ANY_SPEC, VMEM_SPEC, ANY_SPEC, ANY_SPEC, ANY_SPEC) + (VMEM_SPEC,) * 6,
        "decoder_middle",
        scratch=[
            cross.scratch,
            big(ups, n, d, width),
            big(n, rows_of.down_rows, width),
            big(t, 2 * width),
            pltpu.VMEM((t, width), F32),
            big(t, width),
            big(ups, t, width),
            big(ups, t, width),
        ]
        + [pltpu.VMEM((t, width), F32)] * 5
        + [
            big(t, width),
            pltpu.SemaphoreType.DMA((4, 2)),
            pltpu.SemaphoreType.DMA((8 + ups,)),
            pltpu.SemaphoreType.DMA((n,)),
        ],
    )


def put_pieces(refs, i, count, value):
    rows, size = value.shape
    value = value.astype(BF)
    side, at = divmod(i, count // 2)
    for h in range(2):
        refs[2 * h + side][:, at * size : (at + 1) * size] = value[h * rows // 2 : (h + 1) * rows // 2]


def norm_backward(cot, more, normed, inverse, gain, active_rel):
    t, width = cot.shape
    half = active_rel.shape[0] // 2

    def kernel(cot_ref, more_ref, n_ref, i_ref, gain_ref, a_hbm, *refs):
        grad_ref, low_ref, dg_ref, db_ref, *sent_refs, a, sem = refs
        copy = pltpu.make_async_copy(a_hbm.at[pl.ds(0, half)], a, sem)
        copy.start()
        g = cot_ref[...] + more_ref[...].astype(F32)
        dg_ref[...] = jnp.sum(g * n_ref[...], axis=0, keepdims=True)
        db_ref[...] = jnp.sum(g, axis=0, keepdims=True)
        grad = norm_back_values(g, n_ref[...], i_ref[...], gain_ref[...])
        grad_ref[...] = grad
        low_ref[...] = grad.astype(BF)
        copy.wait()

        for h in range(2):

            def step(j):
                value = dot(a[column(2 * h + j, half // 4)], low_ref[...]).astype(BF)
                for c in range(2):
                    sent_refs[2 * h + c][column(j, half // 4)] = value[:, c * width // 2 : (c + 1) * width // 2]

            blocks_loop(2, step)

    vector = shape_of(1, width)
    return kernel_call(
        kernel,
        (shape_of(t, width), shape_of(t, width, BF), vector, vector)
        + (shape_of(half // 2, width // 2, BF),) * 4,
        (cot, more, normed, inverse, gain, active_rel),
        [VMEM_SPEC] * 5 + [ANY_SPEC],
        (VMEM_SPEC,) * 8,
        "norm_backward",
        scratch=[pltpu.VMEM((half, t), BF), pltpu.SemaphoreType.DMA],
    )


def ffn_backward(branch, slope, weights, rows_of, third_rel):
    t, width = branch.shape
    n, d, ups = weights.shape[0], rows_of.d, rows_of.ups
    per = n // ups
    half = width // 2

    def kernel(branch_ref, slope_ref, a_ref, w_hbm, out_ref, d_inner_ref, *refs):
        *sent_refs, w_up, w_down, sems = refs
        down_copies = [
            pltpu.make_async_copy(
                w_hbm.at[pl.ds(i * per, per), pl.ds(rows_of.down, rows_of.down_rows)],
                w_down.at[pl.ds(i * per, per)],
                sems.at[i],
            )
            for i in range(ups)
        ]
        for copy in down_copies:
            copy.start()
        up_copies = [fetch(w_hbm, rows_of.up + i * d, d, w_up.at[i], sems.at[ups + i]) for i in range(ups)]
        for i in range(ups):
            cols = slice(i * width, (i + 1) * width)
            down_copies[i].wait()
            d_act = dot_nt(branch_ref[...], w_down[i * per : (i + 1) * per].reshape(width, width))
            d_inner_ref[:, cols] = (d_act * slope_ref[i].astype(F32)).astype(BF)
            put_pieces(sent_refs, i, ups, dot(a_ref[:half], d_inner_ref[:, cols]))
        for i in range(ups):
            up_copies[i].wait()
            part = dot_nt(
                d_inner_ref[:, i * width : (i + 1) * width], w_up[i].reshape(n * d, width)
            )
            if i == 0:
                out_ref[...] = part
            else:
                out_ref[...] += part

    return kernel_call(
        kernel,
        (shape_of(t, width), shape_of(t, ups * width, BF)) + (shape_of(half // 2, ups * width // 2, BF),) * 4,
        (branch, slope, third_rel, weights),
        [VMEM_SPEC, VMEM_SPEC, VMEM_SPEC, ANY_SPEC],
        (VMEM_SPEC,) * 6,
        "ffn_backward",
        scratch=[
            pltpu.VMEM((ups, n, d, width), BF),
            pltpu.VMEM((n, rows_of.down_rows, width), BF),
            pltpu.SemaphoreType.DMA((2 * ups,)),
        ],
    )


def attention_backward(info, from_dec, third, inner, normed, inverse, gain, weights, rows_of, packed, mask, stack):
    t, width = third.shape
    n, d = weights.shape[0], rows_of.d
    half = width // 2

    def kernel(info_ref, dec_ref, third_ref, inner_ref, n_ref, i_ref, gain_ref, packed_ref, mask_ref, a_ref, w_hbm, *refs):
        grad_ref, d_ref, dg_ref, db_ref, *sent_refs, w_attn, blended, sem = refs
        copy = fetch(w_hbm, rows_of.attn, d, w_attn, sem)
        g = jnp.where(info_ref[1] == 1, dec_ref[...], third_ref[...] + inner_ref[...])
        dg_ref[...] = jnp.sum(g * n_ref[...], axis=0, keepdims=True)
        db_ref[...] = jnp.sum(g, axis=0, keepdims=True)
        grad = norm_back_values(g, n_ref[...], i_ref[...], gain_ref[...])
        grad_ref[...] = grad
        d_ref[:, 3 * width :] = grad.astype(BF)
        copy.wait()
        blended[...] = dot_nt(d_ref[:, 3 * width :], whole(w_attn)).astype(BF)
        attend_back_all(
            blended, packed_ref, 0, packed_ref, width, 2 * width, mask_ref, d_ref, width
        )
        for i in range(4):
            cols = slice(i * width, (i + 1) * width)
            put_pieces(sent_refs, i, 4, dot(a_ref[0 if i < 3 else 1, :half], d_ref[:, cols]))

    wide, vector = shape_of(t, 4 * width, BF), shape_of(1, width)
    return kernel_call(
        kernel,
        (shape_of(t, width), wide, vector, vector) + (shape_of(half // 2, 2 * width, BF),) * 4,
        (info, from_dec, third, inner, normed, inverse, gain, packed, mask, stack, weights),
        [SMEM_SPEC] + [VMEM_SPEC] * 8 + [VMEM_SPEC, ANY_SPEC],
        (VMEM_SPEC,) * 8,
        "attention_backward",
        scratch=[
            pltpu.VMEM((n, d, width), BF),
            pltpu.VMEM((t, width), BF),
            pltpu.SemaphoreType.DMA,
        ],
    )


def embed_backward(grad, d_packed, normed, inverse, gain, weights, rows_of):
    t, width = grad.shape
    n, d = weights.shape[0], rows_of.d

    def kernel(grad_ref, dp_ref, n_ref, i_ref, gain_ref, w_hbm, *refs):
        low_ref, tokens_ref, dg_ref, db_ref, w_qkv, w_in, total, sems = refs
        copies = [fetch(w_hbm, rows_of.qkv + i * d, d, w_qkv.at[i], sems.at[i]) for i in range(3)]
        last = fetch(w_hbm, rows_of.w_in, d, w_in, sems.at[3])
        total[...] = grad_ref[...]
        for i in range(3):
            copies[i].wait()
            total[...] += dot_nt(
                dp_ref[:, i * width : (i + 1) * width], w_qkv[i].reshape(n * d, width)
            )
        g = total[...]
        dg_ref[...] = jnp.sum(g * n_ref[...], axis=0, keepdims=True)
        db_ref[...] = jnp.sum(g, axis=0, keepdims=True)
        low_ref[...] = norm_back_values(g, n_ref[...], i_ref[...], gain_ref[...]).astype(BF)
        last.wait()
        tokens_ref[...] = dot_nt(low_ref[...], whole(w_in))

    vector = shape_of(1, width)
    return kernel_call(
        kernel,
        (shape_of(t, width, BF), shape_of(t, n * d), vector, vector),
        (grad, d_packed, normed, inverse, gain, weights),
        [VMEM_SPEC, VMEM_SPEC] + [VMEM_SPEC] * 3 + [ANY_SPEC],
        (VMEM_SPEC,) * 4,
        "embed_backward",
        scratch=[
            pltpu.VMEM((3, n, d, width), BF),
            pltpu.VMEM((n, d, width), BF),
            pltpu.VMEM((t, width), F32),
            pltpu.SemaphoreType.DMA((4,)),
        ],
    )


def outer(a, first, count, dy, *adds, picks=(), pieces=False, columns=None):
    t = dy.shape[0]
    start, width = columns or (0, dy.shape[1])
    block = min(width if columns else width // 2, 1024)
    grid = width // block
    mid = grid // 2
    per = grid // max(len(picks), 1)
    stacked = a.ndim == 3
    low = lambda j: jnp.minimum(j, mid - 1)
    high = lambda j: jnp.maximum(j - mid, 0)

    def kernel(a_ref, dy_ref, *refs):
        j = pl.program_id(0)
        value = dot(a_ref[0] if stacked else a_ref[...], dy_ref[...])
        outs = refs[sum(len(parts) for parts, _ in adds) :]
        for parts, _ in adds:
            terms, refs = [ref[...].astype(F32) for ref in refs[: len(parts)]], refs[len(parts) :]
            value = value + (jnp.where(j < mid, *terms) if len(terms) == 2 else terms[0])
        value = value.astype(BF)
        if not pieces:
            outs[0][...] = value
            return

        @pl.when(j < mid)
        def _():
            outs[0][...] = value[: count // 2]
            outs[2][...] = value[count // 2 :]

        @pl.when(j >= mid)
        def _():
            outs[1][...] = value[: count // 2]
            outs[3][...] = value[count // 2 :]

    if stacked:
        pick = lambda j: sum(jnp.where(j // per == i, at, 0) for i, at in enumerate(picks))
        a_spec = pl.BlockSpec((1, count, t), lambda j: (pick(j), first // count, 0))
    else:
        a_spec = pl.BlockSpec((count, t), lambda j: (first // count, 0))
    specs = [a_spec, pl.BlockSpec((t, block), lambda j: (0, start // block + j))]
    for parts, at in adds:
        for place in (low, high) if len(parts) == 2 else (lambda j: j,):
            specs.append(pl.BlockSpec((count, block), lambda j, at=at, place=place: (at // count, place(j))))
    if pieces:
        out_specs = [pl.BlockSpec((count // 2, block), lambda j, place=place: (0, place(j))) for place in (low, high)] * 2
        out_shape = [jax.ShapeDtypeStruct((count // 2, width // 2), BF)] * 4
    else:
        out_specs = pl.BlockSpec((count, block), lambda j: (0, j))
        out_shape = jax.ShapeDtypeStruct((count, width), BF)
    return pl.pallas_call(
        kernel,
        grid=(grid,),
        in_specs=specs,
        out_specs=out_specs,
        out_shape=out_shape,
        compiler_params=pltpu.CompilerParams(vmem_limit_bytes=VMEM_LIMIT),
        cost_estimate=pl.CostEstimate(flops=0, bytes_accessed=0, transcendentals=0),
        name="outer",
    )(a, dy, *[part for parts, _ in adds for part in parts])


def shards(
    section_in,
    segment_ids,
    out_cot,
    in_proj,
    attn_in,
    attn_out,
    ffn_in,
    ffn_out,
    norm_gain,
    norm_bias,
    cross_in,
    cross_out,
    cross_gain,
    cross_bias,
):
    n = lax.axis_size("dp")
    me = lax.axis_index("dp")
    is_dec = lax.axis_index("section") == 1
    width = attn_out.shape[2]
    inner_width = ffn_in.shape[2]
    d_loc = attn_out.shape[1]
    in_loc = in_proj.shape[1]
    c_loc = cross_in.shape[0]
    m = n // 4
    depth = d_loc * n

    order = relative_blocks(me, n)
    places = jnp.sum(jnp.arange(n)[:, None] * (order[:, None] == jnp.arange(n)[None, :]), axis=0)
    info = jnp.concatenate([jnp.stack([me, lax.axis_index("section")]), places]).astype(jnp.int32)

    rows_of = Rows(d_loc, inner_width, width)
    params = jnp.concatenate(
        [norm_gain[0].reshape(-1), norm_bias[0].reshape(-1), cross_gain, cross_bias]
    )
    n_par = params.shape[0]

    def columns_of(w):
        return [w[:, i * width : (i + 1) * width] for i in range(w.shape[1] // width)]

    pack = [in_proj[0], jnp.pad(params[None], ((0, d_loc - in_loc - 1), (0, width - n_par)))]
    pack += columns_of(attn_in[0]) + [attn_out[0]] + columns_of(ffn_in[0]) + [ffn_out[0]]
    weights = lax.all_gather(jnp.concatenate(pack, axis=0).astype(BF), "dp", axis=0)
    own_cross = jnp.concatenate(columns_of(cross_in) + [cross_out], axis=0).astype(BF)
    cross_pack = jnp.concatenate([to_decoder(own_cross), own_cross], axis=0)
    cross_w = Cross(lax.all_gather(after(cross_pack, weights), "dp", axis=0))

    tokens = section_in[0]
    tokens = tokens.reshape(tokens.shape[0], n, in_loc)
    tokens = jnp.pad(tokens, ((0, 0), (0, 0), (0, d_loc - in_loc))).reshape(-1, depth)
    cot = out_cot[0]
    seqs = tokens.shape[0] // SEQ
    seg = segment_ids.reshape(2, seqs, SEQ)
    own_seg = jnp.where(is_dec, seg[1], seg[0])
    enc_seg = seg[0]
    spots = jnp.arange(SEQ)
    causal = (spots[:, None] <= spots[None, :]) | jnp.logical_not(is_dec)
    self_mask = ((own_seg[:, None, :] == own_seg[:, :, None]) & causal[None]).astype(F32)
    cross_mask = (own_seg[:, None, :] == enc_seg[:, :, None]).astype(F32)
    perm_d = order_matrix(order, d_loc)
    perm_cross = order_matrix(order, c_loc, 2)
    marks = (jnp.arange(depth)[None, :] == (jnp.arange(n) * d_loc + in_loc)[:, None]).astype(BF)
    tokens_rel = reordered(jnp.concatenate([tokens, marks], axis=0), perm_d)

    pars = weights[:, in_loc, :n_par].astype(F32)

    def vectors(at):
        part = pars[:, 3 * at * d_loc : 3 * (at + 1) * d_loc].reshape(n, 3, d_loc)
        part = part.transpose(1, 0, 2).reshape(3, 1, width)
        return [part[i] for i in range(3)]

    gains, biases = vectors(0), vectors(1)
    own_cpar = pars[:, 6 * d_loc :].astype(BF)
    cpar = jnp.stack([to_decoder(own_cpar), own_cpar]).astype(F32)
    c_gain = cpar[:, :, :c_loc].reshape(1, width)
    c_bias = cpar[:, :, c_loc:].reshape(1, width)

    xa, ia, first_low, packed, blended, second, xb, ib, second_low, encoded = front(
        tokens, self_mask, weights, rows_of, gains, biases
    )
    memory = to_decoder(encoded)
    cross_q = cross_query(second_low, cross_w)
    attn_rel = jnp.stack([reordered(first_low, perm_d), reordered(blended, perm_d)])
    second_rel = reordered(second_low, perm_cross)
    cross_q = after(cross_q, attn_rel, second_rel, tokens_rel)

    output, xd, idd, third_low, active_rel, slope, cross_mix, d_cross, d_memory, resid, dg_c, db_c = (
        decoder_middle(
            info,
            memory,
            cross_q,
            second,
            cot,
            cross_mask,
            weights,
            rows_of,
            cross_w,
            c_gain,
            c_bias,
            gains[2],
            biases[2],
        )
    )
    grad_memory = to_encoder(d_memory)
    grad_second_dec = cross_query_back(resid, d_cross, cross_w)
    third_rel = reordered(third_low, perm_d)
    if active_rel.ndim == 3:
        blocks = active_rel.transpose(1, 0, 2).reshape(tokens.shape[0], n, inner_width // n)
        active_rel = blocks[:, order].reshape(tokens.shape[0], inner_width)
    active_rel = active_rel.T
    cross_rel = jnp.stack(
        [second_rel, reordered(memory, perm_cross), reordered(cross_mix, perm_cross)]
    )
    cvec = jnp.concatenate([dg_c, db_c]).astype(BF).reshape(2, 2, n, c_loc)
    cvec_got = to_encoder(cvec[:, 0])
    cot = after(cot, grad_second_dec, third_rel, cross_rel)

    chain = Chain()
    quarter = width // 4
    grad_d, branch_d, dg_d, db_d, *sent = norm_backward(
        cot, grad_memory, xd, idd, gains[2], active_rel
    )
    chain.mark(*sent)
    got = [swap_core(piece) for piece in sent]
    half = width // 2
    down0 = Part(chain, active_rel, branch_d, got[::2], (), (0, half))
    down1 = Part(chain, active_rel, branch_d, got[1::2], (), (half, half))
    cross = Part(chain, cross_rel, d_cross, picks=(0, 1, 1, 2))
    down0.pair()
    grad_inner, d_inner, *sent = ffn_backward(
        chain(branch_d), slope, weights, rows_of, third_rel
    )
    chain.mark(*sent)
    up = Part(chain, third_rel, d_inner, [swap_core(piece) for piece in sent])
    far = cross.outer(2 * quarter, quarter, (cross.got[:2], 0))
    far = to_encoder(after(far, cvec_got))
    down1.pair(down0.pair_got)
    down0.add()
    down0.spread()
    grad_b, d_attn, dg_b, db_b, *sent = attention_backward(
        info,
        grad_second_dec,
        grad_d,
        chain(grad_inner),
        xb,
        ib,
        gains[1],
        weights,
        rows_of,
        packed,
        self_mask,
        attn_rel,
    )
    chain.mark(*sent)
    attn = Part(chain, attn_rel, d_attn, [swap_core(piece) for piece in sent], (0, 0, 0, 1))
    up.pair()
    d_embed, d_tokens, dg_a, db_a = embed_backward(
        grad_b, chain(d_attn), xa, ia, gains[0], weights, rows_of
    )
    chain.mark(d_embed)
    down1.add()
    down1.spread(down0.blocks)
    cvec = jnp.where(is_dec, cvec[:, 1], cvec_got).transpose(1, 0, 2)
    vecs = jnp.concatenate([dg_a, dg_b, dg_d, db_a, db_b, db_d]).astype(BF)
    vecs = vecs.reshape(6, n, d_loc).transpose(1, 0, 2).reshape(n, 6 * d_loc)
    vecs = jnp.concatenate([vecs, cvec.reshape(n, 2 * c_loc)], axis=1)
    vecs = jnp.pad(vecs, ((0, 0), (0, width - n_par)))
    into = Part(chain, tokens_rel, jnp.concatenate([d_embed, vecs], axis=0))
    near = cross.outer(3 * quarter, quarter, (cross.got[2:], 0))
    near = chain.mark(jnp.where(is_dec, near, far))
    cross_pair = swap_pair(near[: quarter // 2])
    attn.pair()
    into.pair()
    up.add()
    up.spread(down1.blocks)
    cross_total = chain.mark(add_low(near[quarter // 2 :], cross_pair))
    cross_blocks = spread_outer(after(cross_total, up.blocks))
    cross_total = summed(cross_blocks)
    attn.add()
    attn.spread(cross_blocks)
    into.add()
    into.spread(attn.blocks)

    in_grad = chain(d_tokens).reshape(-1, n, d_loc)[:, :, :in_loc].reshape(-1, n * in_loc)
    attn_total = attn.total()
    in_total = into.total()
    row = in_total[in_loc]
    gain_total = row[: 3 * d_loc].reshape(1, 3, d_loc)
    bias_total = row[3 * d_loc : 6 * d_loc].reshape(1, 3, d_loc)

    return (
        output[None],
        in_grad[None],
        in_total[:in_loc][None],
        attn_total[None, :, : 3 * width],
        attn_total[None, :, 3 * width :],
        up.total()[None],
        jnp.concatenate([down0.total(), down1.total()], axis=1)[None],
        gain_total,
        bias_total,
        cross_total[:, : 3 * width],
        cross_total[:, 3 * width :],
        row[6 * d_loc : 6 * d_loc + c_loc],
        row[6 * d_loc + c_loc : n_par],
    )


def solution(mesh):
    placed = (
        P("section", "dp", None),
        P(None, "dp"),
        P("section", "dp", None),
        P("section", "dp", None),
        P("section", "dp", None),
        P("section", "dp", None),
        P("section", "dp", None),
        P("section", "dp", None),
        P("section", None, "dp"),
        P("section", None, "dp"),
        P(("section", "dp"), None),
        P(("section", "dp"), None),
        P(("section", "dp")),
        P(("section", "dp")),
    )
    return jax.shard_map(
        shards,
        mesh=mesh,
        in_specs=placed,
        out_specs=(
            P("section", "dp", None),
            P("section", "dp", None),
            P("section", "dp", None),
            P("section", "dp", None),
            P("section", "dp", None),
            P("section", "dp", None),
            P("section", "dp", None),
            P("section", None, "dp"),
            P("section", None, "dp"),
            P(("section", "dp"), None),
            P(("section", "dp"), None),
            P(("section", "dp")),
            P(("section", "dp")),
        ),
        check_vma=False,
    )
```

```python
import math

import jax
import jax.numpy as jnp
from jax import lax
from jax.experimental import pallas as pl
from jax.experimental.pallas import tpu as pltpu
from jax.sharding import PartitionSpec as P

HEAD_DIM = 64
SEQ = 128
NEG_FILL = -1000000000.0
BF = jnp.bfloat16
F32 = jnp.float32


def swap_core(x):
    n = lax.axis_size("dp")
    return lax.ppermute(x, "dp", [(i, i ^ 1) for i in range(n)])


def swap_pair(x):
    n = lax.axis_size("dp")
    return lax.ppermute(x, "dp", [(i, i ^ 2) for i in range(n)])


def spread_outer(x):
    n = lax.axis_size("dp")
    groups = [list(range(at, n, 4)) for at in range(4)]
    x = x.reshape(n // 4, -1, x.shape[1])
    return lax.all_to_all(x, "dp", 0, 0, axis_index_groups=groups)


def shift_outer(x):
    n = lax.axis_size("dp")
    return lax.ppermute(x, "dp", [(i, (i + 4) % n) for i in range(n)])


def gather_by_steps(x):
    pieces = [x]
    for _ in range(lax.axis_size("dp") // 4 - 1):
        pieces.append(shift_outer(pieces[-1]))
    own = jnp.stack(pieces)
    pair = swap_pair(own)
    return jnp.stack([own, pair], axis=1), jnp.stack([to_decoder(own), to_decoder(pair)], axis=1)


def to_decoder(x):
    return lax.ppermute(x, "section", [(0, 1)])


def to_encoder(x):
    return lax.ppermute(x, "section", [(1, 0)])


def after(x, *deps):
    return lax.optimization_barrier((x,) + deps)[0]


def relative_blocks(me, n):
    m = n // 4
    blk = jnp.arange(n)
    crel = 1 - blk // (2 * m)
    xrel = 1 - (blk % (2 * m)) // m
    return (blk % m) * 4 + ((me // 2) % 2 ^ xrel) * 2 + (me % 2 ^ crel)


def order_matrix(order, block, halves=1):
    n = order.shape[0]
    base = order.reshape(2, 1, n // 2, 1) * block
    src = (
        base
        + jnp.arange(halves).reshape(1, halves, 1, 1) * (n * block)
        + jnp.arange(block).reshape(1, 1, 1, block)
    ).reshape(-1)
    return (jnp.arange(src.shape[0])[:, None] == src[None, :]).astype(BF)


def reordered(a, matrix):
    return jnp.einsum("tk,kr->rt", a, matrix, preferred_element_type=F32).astype(BF)


class Chain:
    def __init__(self):
        self.last = ()

    def __call__(self, x):
        return after(x, *self.last) if self.last else x

    def mark(self, *outs):
        self.last = outs
        return outs[0]


def add_low(a, b):
    return (a.astype(F32) + b.astype(F32)).astype(BF)


def summed(blocks):
    return jnp.sum(blocks.astype(F32), axis=0)


class Part:
    def __init__(self, chain, a, dy, got=None, picks=(), columns=None):
        self.chain, self.a, self.dy, self.picks, self.columns = chain, a, dy, picks, columns
        self.k = a.shape[-2]
        self.got = got or [swap_core(piece) for piece in self.outer(0, self.k // 2, pieces=True)]

    def outer(self, first, count, *adds, pieces=False):
        dy = self.chain(self.dy)
        kinds = {"picks": self.picks, "pieces": pieces, "columns": self.columns}
        made = outer(self.a, first, count, dy, *adds, **kinds)
        self.chain.mark(*(made if pieces else (made,)))
        return made

    def pair(self, *deps):
        q, mid = self.k // 4, len(self.got) // 2
        half = self.outer(2 * q, q, (self.got[:mid], 0))
        self.pair_got = swap_pair(after(half, *deps) if deps else half)

    def add(self):
        q, mid = self.k // 4, len(self.got) // 2
        self.mine = self.outer(3 * q, q, (self.got[mid:], 0), ((self.pair_got,), 0))

    def spread(self, *deps):
        self.blocks = spread_outer(after(self.mine, *deps) if deps else self.mine)

    def total(self):
        return summed(self.blocks)


VMEM_LIMIT = 58 * 2**20


def dot(a, b):
    return jnp.dot(a, b, preferred_element_type=F32)


def dot_nt(a, b):
    return lax.dot_general(a, b, (((1,), (1,)), ((), ())), preferred_element_type=F32)


def dot_tn(a, b):
    return lax.dot_general(a, b, (((0,), (0,)), ((), ())), preferred_element_type=F32)


SMEM_SPEC = pl.BlockSpec(memory_space=pltpu.SMEM)
VMEM_SPEC = pl.BlockSpec(memory_space=pltpu.VMEM)
ANY_SPEC = pl.BlockSpec(memory_space=pl.ANY)


def shape_of(rows, columns, dtype=F32):
    return jax.ShapeDtypeStruct((rows, columns), dtype)


def kernel_call(body, out_shape, args, specs, out_specs, name, scratch=(), cost=0):
    return pl.pallas_call(
        body,
        in_specs=specs,
        out_specs=out_specs,
        out_shape=out_shape,
        scratch_shapes=scratch,
        compiler_params=pltpu.CompilerParams(vmem_limit_bytes=VMEM_LIMIT),
        cost_estimate=pl.CostEstimate(flops=cost, bytes_accessed=0, transcendentals=0),
        name=name,
    )(*args)


class Rows:
    def __init__(self, d_loc, inner_width, width):
        self.d = d_loc
        self.width = width
        self.ups = inner_width // width
        self.down_rows = self.ups * d_loc
        self.w_in = 0
        self.qkv = d_loc
        self.attn = 4 * d_loc
        self.up = 5 * d_loc
        self.down = self.up + self.ups * d_loc


def fetch(src, row, rows, dst, sem):
    copy = pltpu.make_async_copy(src.at[:, pl.ds(row, rows)], dst, sem)
    copy.start()
    return copy


def whole(ref):
    value = ref[...]
    return value.reshape(value.shape[0] * value.shape[1], value.shape[2])


def halves(x):
    low_half = lax.broadcasted_iota(jnp.int32, x.shape, 1) < HEAD_DIM
    zero = jnp.zeros_like(x)
    return jnp.where(low_half, x, zero), jnp.where(low_half, zero, x)


def joined(x):
    rows = x.shape[0] // 2
    low_half = lax.broadcasted_iota(jnp.int32, (rows, x.shape[1]), 1) < HEAD_DIM
    return jnp.where(low_half, x[:rows], x[rows:])


def stacked_heads(x):
    return jnp.concatenate(halves(x), axis=0)


def softmax_t(scores, mask):
    logits = jnp.where(mask[None], scores, NEG_FILL)
    e = jnp.exp(logits - jnp.max(logits, axis=1, keepdims=True))
    return e * (1.0 / jnp.sum(e, axis=1, keepdims=True))


FACTOR = HEAD_DIM ** (-0.5)


def probabilities(q, k_stack, mask):
    scores = dot_nt(k_stack, q * jnp.asarray(FACTOR, BF))
    return softmax_t(scores.reshape((2,) + mask.shape), mask)


def attend_lanes(q, k, v, mask):
    probs = probabilities(q, stacked_heads(k), mask).astype(BF)
    return dot_tn(probs.reshape(2 * SEQ, SEQ), stacked_heads(v)).astype(BF)


def attend_back_lanes(g, q, k, v, mask):
    k_stack = stacked_heads(k)
    probs = probabilities(q, k_stack, mask)
    d_probs = dot_nt(stacked_heads(v), g).reshape(probs.shape)
    centred = jnp.sum(probs * d_probs, axis=1, keepdims=True)
    d_s = (probs * (d_probs - centred) * FACTOR).astype(BF).reshape(2 * SEQ, SEQ)
    d_v = joined(dot(probs.astype(BF).reshape(2 * SEQ, SEQ), g))
    d_k = joined(dot(d_s, q))
    return [part.astype(BF) for part in (dot_tn(d_s, k_stack), d_k, d_v)]


def lanes_of(i, offset=0):
    return pl.ds(pl.multiple_of(offset + i * 128, 128), 128)


def attend_all(q_ref, q_at, kv_ref, k_at, v_at, mask_ref, out_ref, width):
    rows = q_ref.shape[0]

    def step(i, carry):
        for b in range(rows // SEQ):
            s = pl.ds(b * SEQ, SEQ)
            out_ref[s, lanes_of(i)] = attend_lanes(
                q_ref[s, lanes_of(i, q_at)],
                kv_ref[s, lanes_of(i, k_at)],
                kv_ref[s, lanes_of(i, v_at)],
                mask_ref[b] > 0,
            )
        return carry

    lax.fori_loop(0, width // 128, step, 0, unroll=4)


def attend_back_all(g_ref, q_ref, q_at, kv_ref, k_at, v_at, mask_ref, out_ref, width):
    rows = g_ref.shape[0]

    def step(i, carry):
        for b in range(rows // SEQ):
            s = pl.ds(b * SEQ, SEQ)
            parts = attend_back_lanes(
                g_ref[s, lanes_of(i)],
                q_ref[s, lanes_of(i, q_at)],
                kv_ref[s, lanes_of(i, k_at)],
                kv_ref[s, lanes_of(i, v_at)],
                mask_ref[b] > 0,
            )
            for at, part in enumerate(parts):
                out_ref[s, lanes_of(i, at * width)] = part
        return carry

    lax.fori_loop(0, width // 128, step, 0, unroll=4)


def norm_values(values, gain, bias):
    centre = values - jnp.mean(values, axis=-1, keepdims=True)
    inverse = lax.rsqrt(jnp.mean(centre * centre, axis=-1, keepdims=True) + 1e-05)
    normed = centre * inverse
    return normed * gain + bias, normed, inverse


def norm_back_values(upstream, normed, inverse, gain):
    scaled = upstream * gain
    return inverse * (
        scaled
        - jnp.mean(scaled, axis=-1, keepdims=True)
        - normed * jnp.mean(scaled * normed, axis=-1, keepdims=True)
    )


def gelu_parts(inner, with_slope):
    erf = 1.0 + lax.erf(inner * (1.0 / math.sqrt(2.0)))
    active = (0.5 * inner * erf).astype(BF)
    if not with_slope:
        return active
    bell = jnp.exp(-0.5 * inner * inner) * (1.0 / math.sqrt(2.0 * math.pi))
    return active, (0.5 * erf + inner * bell).astype(BF)


BLOCK = 512


def column(j, size=BLOCK):
    return pl.ds(pl.multiple_of(j * size, size), size)


def blocks_loop(count, step):
    lax.fori_loop(0, count, lambda j, carry: (step(j), carry)[1], 0)


def front(tokens, mask, weights, rows_of, gains, biases):
    t = tokens.shape[0]
    n, _, width = weights.shape
    d, ups = rows_of.d, rows_of.ups
    inner_width = ups * width

    def kernel(x_ref, mask_ref, g0, g1, g2, b0, b1, b2, w_hbm, *refs):
        xa_hbm, ia_ref, first_hbm, packed_hbm, mix_hbm, second_hbm, xb_hbm, ib_ref, second_low_hbm, memory_ref = refs[:10]
        w_in, w_qkv, w_attn, w_up, w_down, held, normed, low, packed, mix, second_low, total, active = refs[10:23]
        sems, out_sems = refs[23:]
        first_copy = fetch(w_hbm, rows_of.w_in, d, w_in, sems.at[0])
        qkv_copies = [fetch(w_hbm, rows_of.qkv + i * d, d, w_qkv.at[i], sems.at[1 + i]) for i in range(3)]
        attn_copy = fetch(w_hbm, rows_of.attn, d, w_attn, sems.at[4])
        up_copies = [fetch(w_hbm, rows_of.up + i * d, d, w_up.at[i], sems.at[6 + i]) for i in range(ups)]
        down_copy = fetch(w_hbm, rows_of.down, rows_of.down_rows, w_down, sems.at[5])
        outs = []

        def put(src, dst):
            outs.append(pltpu.make_async_copy(src, dst, out_sems.at[len(outs)]))
            outs[-1].start()

        first_copy.wait()
        first, xa, ia = norm_values(dot(x_ref[...], whole(w_in)), g0[...], b0[...])
        held[...] = first
        normed[...] = xa
        ia_ref[...] = ia
        low[...] = first.astype(BF)
        put(normed, xa_hbm)
        put(low, first_hbm)
        for copy in qkv_copies:
            copy.wait()

        def project(j):
            packed[:, column(j, width)] = dot(
                low[...], w_qkv[j].reshape(n * d, width)
            ).astype(BF)

        blocks_loop(3, project)
        put(packed, packed_hbm)
        attend_all(packed, 0, packed, width, 2 * width, mask_ref, mix, width)
        put(mix, mix_hbm)
        attn_copy.wait()
        second, xb, ib = norm_values(held[...] + dot(mix[...], whole(w_attn)), g1[...], b1[...])
        outs[0].wait()
        held[...] = second
        normed[...] = xb
        ib_ref[...] = ib
        second_low[...] = second.astype(BF)
        put(held, second_hbm)
        put(normed, xb_hbm)
        put(second_low, second_low_hbm)
        for copy in up_copies:
            copy.wait()

        def forward(j):
            active[j] = gelu_parts(dot(second_low[...], w_up[j].reshape(n * d, width)), False)

        blocks_loop(ups, forward)
        down_copy.wait()
        total[...] = second

        def forward_down(j):
            rows = pl.ds(j * (n // ups), n // ups)
            total[...] += dot(active[j], w_down[rows].reshape(width, width))

        blocks_loop(ups, forward_down)
        memory_ref[...] = norm_values(total[...], g2[...], b2[...])[0].astype(BF)
        for copy in outs[1:]:
            copy.wait()

    value, low, vector = shape_of(t, width), shape_of(t, width, BF), shape_of(t, 1)
    big = lambda *shape: pltpu.VMEM(shape, BF)
    return kernel_call(
        kernel,
        (value, vector, low, shape_of(t, 3 * width, BF), low, value, value, vector, low, low),
        (tokens, mask, *gains, *biases, weights),
        [VMEM_SPEC] * 8 + [ANY_SPEC],
        (ANY_SPEC, VMEM_SPEC) + (ANY_SPEC,) * 5 + (VMEM_SPEC, ANY_SPEC, VMEM_SPEC),
        "front",
        scratch=[
            big(n, d, width),
            big(3, n, d, width),
            big(n, d, width),
            big(ups, n, d, width),
            big(n, rows_of.down_rows, width),
            pltpu.VMEM((t, width), F32),
            pltpu.VMEM((t, width), F32),
            big(t, width),
            big(t, 3 * width),
            big(t, width),
            big(t, width),
            pltpu.VMEM((t, width), F32),
            big(ups, t, width),
            pltpu.SemaphoreType.DMA((6 + ups,)),
            pltpu.SemaphoreType.DMA((7,)),
        ],
    )


def arrivals(me, m):
    z, x, core = me // 4, lax.rem(me // 2, 2), lax.rem(me, 2)
    for h in range(2):
        for k in range(m):
            for xrel in range(2):
                outer_pair = lax.rem(z - k + m, m) * 4 + lax.rem(x + xrel, 2) * 2
                yield h, k, xrel, outer_pair + lax.rem(core + h, 2)


class Cross:
    def __init__(self, far, own, me):
        m, _, _, self.c, self.width = own.shape
        self.m, self.n = m, 4 * m
        self.arrays = (far, swap_core(far), own, swap_core(own))
        if self.c % 16:
            index = jnp.stack([j for *_, j in arrivals(me, self.m)])
            back = jnp.sum((index[:, None] == jnp.arange(self.n)) * jnp.arange(self.n)[:, None], axis=0)
            sections = []
            for one, other in (self.arrays[:2], self.arrays[2:]):
                both = jnp.stack([one, other]).reshape(self.n, 4, self.c, self.width)
                sections.append(both[back])
            self.arrays = (jnp.stack(sections).transpose(2, 0, 1, 3, 4),)

    @property
    def specs(self):
        return [ANY_SPEC] * len(self.arrays)

    @property
    def scratch(self):
        return [pltpu.VMEM((4, 2, self.n, self.c, self.width), BF), pltpu.SemaphoreType.DMA((2, 2, self.n))]

    def start(self, refs, dst, sems, me, first, count):
        groups = pl.ds(first, count)
        if len(refs) == 1:
            copies = [pltpu.make_async_copy(refs[0].at[groups], dst.at[groups], sems.at[0, 0])]
        else:
            copies = [
                pltpu.make_async_copy(
                    refs[2 * s + h].at[k, xrel, groups], dst.at[groups, s, j], sems.at[s, i]
                )
                for i, (h, k, xrel, j) in enumerate(arrivals(me, self.m))
                for s in range(2)
            ]
        for copy in copies:
            copy.start()
        return copies

    def matrix(self, ref, i):
        return ref[i].reshape(2 * self.n * self.c, self.width)


def cross_query(info, low, cross):
    t, width = low.shape
    count = len(cross.arrays)

    def kernel(info_ref, low_ref, *refs):
        out_ref, w, sems = refs[count:]
        for copy in cross.start(refs[:count], w, sems.at[0], info_ref[0], 0, 1):
            copy.wait()
        out_ref[...] = dot(low_ref[...], cross.matrix(w, 0)).astype(BF)

    return kernel_call(
        kernel,
        shape_of(t, width, BF),
        (info, low, *cross.arrays),
        [SMEM_SPEC, VMEM_SPEC] + cross.specs,
        VMEM_SPEC,
        "cross_query",
        scratch=cross.scratch,
    )


def cross_query_back(info, resid, d_cross, cross):
    t, width = resid.shape
    count = len(cross.arrays)

    def kernel(info_ref, resid_ref, d_ref, *refs):
        out_ref, w, sems = refs[count:]
        for copy in cross.start(refs[:count], w, sems.at[0], info_ref[0], 0, 1):
            copy.wait()
        out_ref[...] = resid_ref[...] + dot_nt(d_ref[:, :width], cross.matrix(w, 0))

    return kernel_call(
        kernel,
        shape_of(t, width),
        (info, resid, d_cross, *cross.arrays),
        [SMEM_SPEC, VMEM_SPEC, VMEM_SPEC] + cross.specs,
        VMEM_SPEC,
        "cross_query_back",
        scratch=cross.scratch,
    )


def decoder_middle(info, memory, cross_q, second, cot, mask, weights, rows_of, cross, c_gain, c_bias, gain, bias):
    t, width = second.shape
    n, d, ups = weights.shape[0], rows_of.d, rows_of.ups
    inner_width = ups * width
    block = inner_width // n
    ordered = block % 128 == 0
    count = len(cross.arrays)
    per = n // ups

    def kernel(info_ref, memory_ref, q_ref, mask_ref, cg_ref, cb_ref, g_ref, b_ref, second_hbm, cot_hbm, w_hbm, *refs):
        c_refs, refs = refs[:count], refs[count:]
        out_hbm, normed_hbm, inv_ref, third_hbm, active_hbm, slope_hbm = refs[:6]
        mix_ref, d_qkv_ref, d_memory_ref, resid_ref, dg_ref, db_ref = refs[6:12]
        w_c, cross_sems, w_up, w_down, kv, third, low, active, slope, out, normed, c_normed, total, cot = refs[12:26]
        d_branch_ref, sems, act_sems = refs[26:]
        is_dec = info_ref[1] == 1
        copies = cross.start(c_refs, w_c, cross_sems.at[0], info_ref[0], 1, 2)
        get_second = pltpu.make_async_copy(second_hbm, third, sems.at[0])
        get_cot = pltpu.make_async_copy(cot_hbm, cot, sems.at[1])
        get_second.start()
        last_copies = cross.start(c_refs, w_c, cross_sems.at[1], info_ref[0], 3, 1)
        up_copies = [fetch(w_hbm, rows_of.up + i * d, d, w_up.at[i], sems.at[8 + i]) for i in range(ups)]
        down_copy = fetch(w_hbm, rows_of.down, rows_of.down_rows, w_down, sems.at[7])
        get_cot.start()
        for copy in copies:
            copy.wait()
        for i in (1, 2):
            kv[:, (i - 1) * width : i * width] = dot(memory_ref[...], cross.matrix(w_c, i)).astype(BF)
        attend_all(q_ref, 0, kv, 0, width, mask_ref, mix_ref, width)
        get_second.wait()
        for copy in last_copies:
            copy.wait()
        values = third[...] + dot(mix_ref[...], cross.matrix(w_c, 3))
        third_c, normed_c, inverse_c = norm_values(values, cg_ref[...], cb_ref[...])
        c_normed[...] = normed_c
        third[...] = jnp.where(is_dec, third_c, third[...])
        low[...] = third[...].astype(BF)
        outs = [pltpu.make_async_copy(low, third_hbm, sems.at[2])]
        outs[-1].start()
        for copy in up_copies:
            copy.wait()

        def forward(j):
            active[j], slope[j] = gelu_parts(dot(low[...], w_up[j].reshape(n * d, width)), True)

        blocks_loop(ups, forward)
        if not ordered:
            outs.append(pltpu.make_async_copy(active, active_hbm, act_sems.at[0]))
            outs[-1].start()
        for j in range(n if ordered else 0):
            place = info_ref[2 + j]
            outs.append(
                pltpu.make_async_copy(
                    active.at[j // per, :, pl.ds((j % per) * block, block)],
                    active_hbm.at[:, column(place, block)],
                    act_sems.at[j],
                )
            )
            outs[-1].start()
        outs.append(pltpu.make_async_copy(slope, slope_hbm, sems.at[4]))
        outs[-1].start()
        down_copy.wait()
        total[...] = third[...]

        def forward_down(j):
            total[...] += dot(active[j], w_down[pl.ds(j * per, per)].reshape(width, width))

        blocks_loop(ups, forward_down)
        last, normed_d, inverse_d = norm_values(total[...], g_ref[...], b_ref[...])
        out[...] = last
        normed[...] = normed_d
        inv_ref[...] = inverse_d
        outs += [
            pltpu.make_async_copy(out, out_hbm, sems.at[5]),
            pltpu.make_async_copy(normed, normed_hbm, sems.at[6]),
        ]
        outs[-2].start()
        outs[-1].start()
        get_cot.wait()
        grad = norm_back_values(cot[...], normed_d, inverse_d, g_ref[...])
        total[...] = grad
        d_branch_ref[...] = grad.astype(BF)

        def backward(j):
            d_act = dot_nt(d_branch_ref[...], w_down[pl.ds(j * per, per)].reshape(width, width))
            d_inner = (d_act * slope[j].astype(F32)).astype(BF)
            total[...] += dot_nt(d_inner, w_up[j].reshape(n * d, width))

        blocks_loop(ups, backward)
        grad = total[...]
        dg_ref[...] = jnp.sum(grad * c_normed[...], axis=0, keepdims=True)
        db_ref[...] = jnp.sum(grad, axis=0, keepdims=True)
        resid = norm_back_values(grad, c_normed[...], inverse_c, cg_ref[...])
        resid_ref[...] = resid
        d_branch_ref[...] = resid.astype(BF)
        outs[0].wait()
        low[...] = dot_nt(d_branch_ref[...], cross.matrix(w_c, 3)).astype(BF)
        attend_back_all(low, q_ref, 0, kv, 0, width, mask_ref, d_qkv_ref, width)
        d_qkv_ref[:, 3 * width :] = d_branch_ref[...]
        d_memory = dot_nt(d_qkv_ref[:, width : 2 * width], cross.matrix(w_c, 1))
        d_memory_ref[...] = (
            d_memory + dot_nt(d_qkv_ref[:, 2 * width : 3 * width], cross.matrix(w_c, 2))
        ).astype(BF)
        for copy in outs[1:]:
            copy.wait()

    value, low = shape_of(t, width), shape_of(t, width, BF)
    vector, blocked = shape_of(1, width), jax.ShapeDtypeStruct((ups, t, width), BF)
    big = lambda *shape: pltpu.VMEM(shape, BF)
    return kernel_call(
        kernel,
        (value, value, shape_of(t, 1), low)
        + (shape_of(t, inner_width, BF) if ordered else blocked, blocked)
        + (low, shape_of(t, 4 * width, BF), low, value, vector, vector),
        (info, memory, cross_q, mask, c_gain, c_bias, gain, bias, second, cot, weights, *cross.arrays),
        [SMEM_SPEC] + [VMEM_SPEC] * 7 + [ANY_SPEC] * 3 + cross.specs,
        (ANY_SPEC, ANY_SPEC, VMEM_SPEC, ANY_SPEC, ANY_SPEC, ANY_SPEC) + (VMEM_SPEC,) * 6,
        "decoder_middle",
        scratch=cross.scratch
        + [
            big(ups, n, d, width),
            big(n, rows_of.down_rows, width),
            big(t, 2 * width),
            pltpu.VMEM((t, width), F32),
            big(t, width),
            big(ups, t, width),
            big(ups, t, width),
        ]
        + [pltpu.VMEM((t, width), F32)] * 5
        + [
            big(t, width),
            pltpu.SemaphoreType.DMA((8 + ups,)),
            pltpu.SemaphoreType.DMA((n,)),
        ],
    )


def put_pieces(refs, i, count, value):
    rows, size = value.shape
    value = value.astype(BF)
    side, at = divmod(i, count // 2)
    for h in range(2):
        refs[2 * h + side][:, at * size : (at + 1) * size] = value[h * rows // 2 : (h + 1) * rows // 2]


def norm_backward(cot, more, normed, inverse, gain, active_rel):
    t, width = cot.shape
    half = active_rel.shape[0] // 2

    def kernel(cot_ref, more_ref, n_ref, i_ref, gain_ref, a_hbm, *refs):
        grad_ref, low_ref, dg_ref, db_ref, *sent_refs, a, sem = refs
        copy = pltpu.make_async_copy(a_hbm.at[pl.ds(0, half)], a, sem)
        copy.start()
        g = cot_ref[...] + more_ref[...].astype(F32)
        dg_ref[...] = jnp.sum(g * n_ref[...], axis=0, keepdims=True)
        db_ref[...] = jnp.sum(g, axis=0, keepdims=True)
        grad = norm_back_values(g, n_ref[...], i_ref[...], gain_ref[...])
        grad_ref[...] = grad
        low_ref[...] = grad.astype(BF)
        copy.wait()

        for h in range(2):

            def step(j):
                value = dot(a[column(2 * h + j, half // 4)], low_ref[...]).astype(BF)
                for c in range(2):
                    sent_refs[2 * h + c][column(j, half // 4)] = value[:, c * width // 2 : (c + 1) * width // 2]

            blocks_loop(2, step)

    vector = shape_of(1, width)
    return kernel_call(
        kernel,
        (shape_of(t, width), shape_of(t, width, BF), vector, vector)
        + (shape_of(half // 2, width // 2, BF),) * 4,
        (cot, more, normed, inverse, gain, active_rel),
        [VMEM_SPEC] * 5 + [ANY_SPEC],
        (VMEM_SPEC,) * 8,
        "norm_backward",
        scratch=[pltpu.VMEM((half, t), BF), pltpu.SemaphoreType.DMA],
    )


def ffn_backward(branch, slope, weights, rows_of, third_rel):
    t, width = branch.shape
    n, d, ups = weights.shape[0], rows_of.d, rows_of.ups
    per = n // ups
    half = width // 2

    def kernel(branch_ref, slope_ref, a_ref, w_hbm, out_ref, d_inner_ref, *refs):
        *sent_refs, w_up, w_down, sems = refs
        down_copies = [
            pltpu.make_async_copy(
                w_hbm.at[pl.ds(i * per, per), pl.ds(rows_of.down, rows_of.down_rows)],
                w_down.at[pl.ds(i * per, per)],
                sems.at[i],
            )
            for i in range(ups)
        ]
        for copy in down_copies:
            copy.start()
        up_copies = [fetch(w_hbm, rows_of.up + i * d, d, w_up.at[i], sems.at[ups + i]) for i in range(ups)]
        for i in range(ups):
            cols = slice(i * width, (i + 1) * width)
            down_copies[i].wait()
            d_act = dot_nt(branch_ref[...], w_down[i * per : (i + 1) * per].reshape(width, width))
            d_inner_ref[:, cols] = (d_act * slope_ref[i].astype(F32)).astype(BF)
            put_pieces(sent_refs, i, ups, dot(a_ref[:half], d_inner_ref[:, cols]))
        for i in range(ups):
            up_copies[i].wait()
            part = dot_nt(
                d_inner_ref[:, i * width : (i + 1) * width], w_up[i].reshape(n * d, width)
            )
            if i == 0:
                out_ref[...] = part
            else:
                out_ref[...] += part

    return kernel_call(
        kernel,
        (shape_of(t, width), shape_of(t, ups * width, BF)) + (shape_of(half // 2, ups * width // 2, BF),) * 4,
        (branch, slope, third_rel, weights),
        [VMEM_SPEC, VMEM_SPEC, VMEM_SPEC, ANY_SPEC],
        (VMEM_SPEC,) * 6,
        "ffn_backward",
        scratch=[
            pltpu.VMEM((ups, n, d, width), BF),
            pltpu.VMEM((n, rows_of.down_rows, width), BF),
            pltpu.SemaphoreType.DMA((2 * ups,)),
        ],
    )


def attention_backward(info, from_dec, third, inner, normed, inverse, gain, weights, rows_of, packed, mask, stack):
    t, width = third.shape
    n, d = weights.shape[0], rows_of.d
    half = width // 2

    def kernel(info_ref, dec_ref, third_ref, inner_ref, n_ref, i_ref, gain_ref, packed_ref, mask_ref, a_ref, w_hbm, *refs):
        grad_ref, d_ref, dg_ref, db_ref, *sent_refs, w_attn, blended, sem = refs
        copy = fetch(w_hbm, rows_of.attn, d, w_attn, sem)
        g = jnp.where(info_ref[1] == 1, dec_ref[...], third_ref[...] + inner_ref[...])
        dg_ref[...] = jnp.sum(g * n_ref[...], axis=0, keepdims=True)
        db_ref[...] = jnp.sum(g, axis=0, keepdims=True)
        grad = norm_back_values(g, n_ref[...], i_ref[...], gain_ref[...])
        grad_ref[...] = grad
        d_ref[:, 3 * width :] = grad.astype(BF)
        copy.wait()
        blended[...] = dot_nt(d_ref[:, 3 * width :], whole(w_attn)).astype(BF)
        attend_back_all(
            blended, packed_ref, 0, packed_ref, width, 2 * width, mask_ref, d_ref, width
        )
        for i in range(4):
            cols = slice(i * width, (i + 1) * width)
            put_pieces(sent_refs, i, 4, dot(a_ref[0 if i < 3 else 1, :half], d_ref[:, cols]))

    wide, vector = shape_of(t, 4 * width, BF), shape_of(1, width)
    return kernel_call(
        kernel,
        (shape_of(t, width), wide, vector, vector) + (shape_of(half // 2, 2 * width, BF),) * 4,
        (info, from_dec, third, inner, normed, inverse, gain, packed, mask, stack, weights),
        [SMEM_SPEC] + [VMEM_SPEC] * 8 + [VMEM_SPEC, ANY_SPEC],
        (VMEM_SPEC,) * 8,
        "attention_backward",
        scratch=[
            pltpu.VMEM((n, d, width), BF),
            pltpu.VMEM((t, width), BF),
            pltpu.SemaphoreType.DMA,
        ],
    )


def embed_backward(grad, d_packed, normed, inverse, gain, weights, rows_of):
    t, width = grad.shape
    n, d = weights.shape[0], rows_of.d

    def kernel(grad_ref, dp_ref, n_ref, i_ref, gain_ref, w_hbm, *refs):
        low_ref, tokens_ref, dg_ref, db_ref, w_qkv, w_in, total, sems = refs
        copies = [fetch(w_hbm, rows_of.qkv + i * d, d, w_qkv.at[i], sems.at[i]) for i in range(3)]
        last = fetch(w_hbm, rows_of.w_in, d, w_in, sems.at[3])
        total[...] = grad_ref[...]
        for i in range(3):
            copies[i].wait()
            total[...] += dot_nt(
                dp_ref[:, i * width : (i + 1) * width], w_qkv[i].reshape(n * d, width)
            )
        g = total[...]
        dg_ref[...] = jnp.sum(g * n_ref[...], axis=0, keepdims=True)
        db_ref[...] = jnp.sum(g, axis=0, keepdims=True)
        low_ref[...] = norm_back_values(g, n_ref[...], i_ref[...], gain_ref[...]).astype(BF)
        last.wait()
        tokens_ref[...] = dot_nt(low_ref[...], whole(w_in))

    vector = shape_of(1, width)
    return kernel_call(
        kernel,
        (shape_of(t, width, BF), shape_of(t, n * d), vector, vector),
        (grad, d_packed, normed, inverse, gain, weights),
        [VMEM_SPEC, VMEM_SPEC] + [VMEM_SPEC] * 3 + [ANY_SPEC],
        (VMEM_SPEC,) * 4,
        "embed_backward",
        scratch=[
            pltpu.VMEM((3, n, d, width), BF),
            pltpu.VMEM((n, d, width), BF),
            pltpu.VMEM((t, width), F32),
            pltpu.SemaphoreType.DMA((4,)),
        ],
    )


def outer(a, first, count, dy, *adds, picks=(), pieces=False, columns=None):
    t = dy.shape[0]
    start, width = columns or (0, dy.shape[1])
    block = min(width if columns else width // 2, 1024)
    grid = width // block
    mid = grid // 2
    per = grid // max(len(picks), 1)
    stacked = a.ndim == 3
    low = lambda j: jnp.minimum(j, mid - 1)
    high = lambda j: jnp.maximum(j - mid, 0)

    def kernel(a_ref, dy_ref, *refs):
        j = pl.program_id(0)
        value = dot(a_ref[0] if stacked else a_ref[...], dy_ref[...])
        outs = refs[sum(len(parts) for parts, _ in adds) :]
        for parts, _ in adds:
            terms, refs = [ref[...].astype(F32) for ref in refs[: len(parts)]], refs[len(parts) :]
            value = value + (jnp.where(j < mid, *terms) if len(terms) == 2 else terms[0])
        value = value.astype(BF)
        if not pieces:
            outs[0][...] = value
            return

        @pl.when(j < mid)
        def _():
            outs[0][...] = value[: count // 2]
            outs[2][...] = value[count // 2 :]

        @pl.when(j >= mid)
        def _():
            outs[1][...] = value[: count // 2]
            outs[3][...] = value[count // 2 :]

    if stacked:
        pick = lambda j: sum(jnp.where(j // per == i, at, 0) for i, at in enumerate(picks))
        a_spec = pl.BlockSpec((1, count, t), lambda j: (pick(j), first // count, 0))
    else:
        a_spec = pl.BlockSpec((count, t), lambda j: (first // count, 0))
    specs = [a_spec, pl.BlockSpec((t, block), lambda j: (0, start // block + j))]
    for parts, at in adds:
        for place in (low, high) if len(parts) == 2 else (lambda j: j,):
            specs.append(pl.BlockSpec((count, block), lambda j, at=at, place=place: (at // count, place(j))))
    if pieces:
        out_specs = [pl.BlockSpec((count // 2, block), lambda j, place=place: (0, place(j))) for place in (low, high)] * 2
        out_shape = [jax.ShapeDtypeStruct((count // 2, width // 2), BF)] * 4
    else:
        out_specs = pl.BlockSpec((count, block), lambda j: (0, j))
        out_shape = jax.ShapeDtypeStruct((count, width), BF)
    return pl.pallas_call(
        kernel,
        grid=(grid,),
        in_specs=specs,
        out_specs=out_specs,
        out_shape=out_shape,
        compiler_params=pltpu.CompilerParams(vmem_limit_bytes=VMEM_LIMIT),
        cost_estimate=pl.CostEstimate(flops=0, bytes_accessed=0, transcendentals=0),
        name="outer",
    )(a, dy, *[part for parts, _ in adds for part in parts])


def shards(
    section_in,
    segment_ids,
    out_cot,
    in_proj,
    attn_in,
    attn_out,
    ffn_in,
    ffn_out,
    norm_gain,
    norm_bias,
    cross_in,
    cross_out,
    cross_gain,
    cross_bias,
):
    n = lax.axis_size("dp")
    me = lax.axis_index("dp")
    is_dec = lax.axis_index("section") == 1
    width = attn_out.shape[2]
    inner_width = ffn_in.shape[2]
    d_loc = attn_out.shape[1]
    in_loc = in_proj.shape[1]
    c_loc = cross_in.shape[0]
    m = n // 4
    depth = d_loc * n

    order = relative_blocks(me, n)
    places = jnp.sum(jnp.arange(n)[:, None] * (order[:, None] == jnp.arange(n)[None, :]), axis=0)
    info = jnp.concatenate([jnp.stack([me, lax.axis_index("section")]), places]).astype(jnp.int32)

    rows_of = Rows(d_loc, inner_width, width)
    params = jnp.concatenate(
        [norm_gain[0].reshape(-1), norm_bias[0].reshape(-1), cross_gain, cross_bias]
    )
    n_par = params.shape[0]

    def columns_of(w):
        return [w[:, i * width : (i + 1) * width] for i in range(w.shape[1] // width)]

    pack = [in_proj[0], jnp.zeros((d_loc - in_loc, width), F32)]
    pack += columns_of(attn_in[0]) + [attn_out[0]] + columns_of(ffn_in[0]) + [ffn_out[0]]
    weights = lax.all_gather(jnp.concatenate(pack, axis=0).astype(BF), "dp", axis=0)
    own_cross = jnp.stack(columns_of(cross_in) + [cross_out]).astype(BF)
    own_cross, far_cross = gather_by_steps(own_cross)
    cross_w = Cross(far_cross, own_cross, me)

    tokens = section_in[0]
    tokens = tokens.reshape(tokens.shape[0], n, in_loc)
    tokens = jnp.pad(tokens, ((0, 0), (0, 0), (0, d_loc - in_loc))).reshape(-1, depth)
    cot = out_cot[0]
    seqs = tokens.shape[0] // SEQ
    seg = segment_ids.reshape(2, seqs, SEQ)
    own_seg = jnp.where(is_dec, seg[1], seg[0])
    enc_seg = seg[0]
    spots = jnp.arange(SEQ)
    causal = (spots[:, None] <= spots[None, :]) | jnp.logical_not(is_dec)
    self_mask = ((own_seg[:, None, :] == own_seg[:, :, None]) & causal[None]).astype(F32)
    cross_mask = (own_seg[:, None, :] == enc_seg[:, :, None]).astype(F32)
    perm_d = order_matrix(order, d_loc)
    perm_cross = order_matrix(order, c_loc, 2)
    marks = (jnp.arange(depth)[None, :] == (jnp.arange(n) * d_loc + in_loc)[:, None]).astype(BF)
    tokens_rel = reordered(jnp.concatenate([tokens, marks], axis=0), perm_d)

    own_pars, far_pars = gather_by_steps(params.astype(BF)[None])
    pars = jnp.stack([far_pars, own_pars]).reshape(2, n // 2, n_par)
    pars = jnp.concatenate([pars, swap_core(pars)], axis=1)
    index = jnp.stack([j for *_, j in arrivals(me, m)])
    place = (jnp.arange(n)[:, None] == index[None, :]).astype(BF)
    pars = jnp.stack([dot(place, pars[0]), dot(place, pars[1])])

    def vectors(at):
        part = pars[1, :, 3 * at * d_loc : 3 * (at + 1) * d_loc].reshape(n, 3, d_loc)
        part = part.transpose(1, 0, 2).reshape(3, 1, width)
        return [part[i] for i in range(3)]

    gains, biases = vectors(0), vectors(1)
    cpar = pars[:, :, 6 * d_loc :]
    c_gain = cpar[:, :, :c_loc].reshape(1, width)
    c_bias = cpar[:, :, c_loc:].reshape(1, width)

    xa, ia, first_low, packed, blended, second, xb, ib, second_low, encoded = front(
        after(tokens, *cross_w.arrays, c_gain, c_bias, perm_d, perm_cross),
        self_mask,
        weights,
        rows_of,
        gains,
        biases,
    )
    memory = to_decoder(encoded)
    cross_q = cross_query(info, second_low, cross_w)
    attn_rel = jnp.stack([reordered(first_low, perm_d), reordered(blended, perm_d)])
    second_rel = reordered(second_low, perm_cross)
    cross_q = after(cross_q, attn_rel, second_rel, tokens_rel)

    output, xd, idd, third_low, active_rel, slope, cross_mix, d_cross, d_memory, resid, dg_c, db_c = (
        decoder_middle(
            info,
            memory,
            cross_q,
            second,
            cot,
            cross_mask,
            weights,
            rows_of,
            cross_w,
            c_gain,
            c_bias,
            gains[2],
            biases[2],
        )
    )
    grad_memory = to_encoder(d_memory)
    grad_second_dec = cross_query_back(info, resid, d_cross, cross_w)
    third_rel = reordered(third_low, perm_d)
    if active_rel.ndim == 3:
        blocks = active_rel.transpose(1, 0, 2).reshape(tokens.shape[0], n, inner_width // n)
        active_rel = blocks[:, order].reshape(tokens.shape[0], inner_width)
    active_rel = active_rel.T
    cross_rel = jnp.stack(
        [second_rel, reordered(memory, perm_cross), reordered(cross_mix, perm_cross)]
    )
    cvec = jnp.concatenate([dg_c, db_c]).astype(BF).reshape(2, 2, n, c_loc)
    cvec_got = to_encoder(cvec[:, 0])
    cot = after(cot, grad_second_dec, third_rel, cross_rel)

    chain = Chain()
    quarter = width // 4
    grad_d, branch_d, dg_d, db_d, *sent = norm_backward(
        cot, grad_memory, xd, idd, gains[2], active_rel
    )
    chain.mark(*sent)
    got = [swap_core(piece) for piece in sent]
    half = width // 2
    down0 = Part(chain, active_rel, branch_d, got[::2], (), (0, half))
    down1 = Part(chain, active_rel, branch_d, got[1::2], (), (half, half))
    cross = Part(chain, cross_rel, d_cross, picks=(0, 1, 1, 2))
    down0.pair()
    grad_inner, d_inner, *sent = ffn_backward(
        chain(branch_d), slope, weights, rows_of, third_rel
    )
    chain.mark(*sent)
    up = Part(chain, third_rel, d_inner, [swap_core(piece) for piece in sent])
    far = cross.outer(2 * quarter, quarter, (cross.got[:2], 0))
    far = to_encoder(after(far, cvec_got))
    down1.pair(down0.pair_got)
    down0.add()
    down0.spread()
    up.pair()
    grad_b, d_attn, dg_b, db_b, *sent = attention_backward(
        info,
        grad_second_dec,
        grad_d,
        chain(grad_inner),
        xb,
        ib,
        gains[1],
        weights,
        rows_of,
        packed,
        self_mask,
        attn_rel,
    )
    chain.mark(*sent)
    attn = Part(chain, attn_rel, d_attn, [swap_core(piece) for piece in sent], (0, 0, 0, 1))
    down1.add()
    down1.spread(down0.blocks)
    d_embed, d_tokens, dg_a, db_a = embed_backward(
        grad_b, chain(d_attn), xa, ia, gains[0], weights, rows_of
    )
    chain.mark(d_embed)
    cvec = jnp.where(is_dec, cvec[:, 1], cvec_got).transpose(1, 0, 2)
    vecs = jnp.concatenate([dg_a, dg_b, dg_d, db_a, db_b, db_d]).astype(BF)
    vecs = vecs.reshape(6, n, d_loc).transpose(1, 0, 2).reshape(n, 6 * d_loc)
    vecs = jnp.concatenate([vecs, cvec.reshape(n, 2 * c_loc)], axis=1)
    vecs = jnp.pad(vecs, ((0, 0), (0, width - n_par)))
    into = Part(chain, tokens_rel, jnp.concatenate([d_embed, vecs], axis=0))
    near = cross.outer(3 * quarter, quarter, (cross.got[2:], 0))
    near = chain.mark(jnp.where(is_dec, near, far))
    cross_pair = swap_pair(near[: quarter // 2])
    attn.pair()
    into.pair()
    up.add()
    up.spread(down1.blocks)
    cross_total = chain.mark(add_low(near[quarter // 2 :], cross_pair))
    cross_blocks = spread_outer(after(cross_total, up.blocks))
    cross_total = summed(cross_blocks)
    attn.add()
    attn.spread(cross_blocks)
    into.add()
    into.spread(attn.blocks)

    in_grad = chain(d_tokens).reshape(-1, n, d_loc)[:, :, :in_loc].reshape(-1, n * in_loc)
    attn_total = attn.total()
    in_total = into.total()
    row = in_total[in_loc]
    gain_total = row[: 3 * d_loc].reshape(1, 3, d_loc)
    bias_total = row[3 * d_loc : 6 * d_loc].reshape(1, 3, d_loc)

    return (
        output[None],
        in_grad[None],
        in_total[:in_loc][None],
        attn_total[None, :, : 3 * width],
        attn_total[None, :, 3 * width :],
        up.total()[None],
        jnp.concatenate([down0.total(), down1.total()], axis=1)[None],
        gain_total,
        bias_total,
        cross_total[:, : 3 * width],
        cross_total[:, 3 * width :],
        row[6 * d_loc : 6 * d_loc + c_loc],
        row[6 * d_loc + c_loc : n_par],
    )


def solution(mesh):
    placed = (
        P("section", "dp", None),
        P(None, "dp"),
        P("section", "dp", None),
        P("section", "dp", None),
        P("section", "dp", None),
        P("section", "dp", None),
        P("section", "dp", None),
        P("section", "dp", None),
        P("section", None, "dp"),
        P("section", None, "dp"),
        P(("section", "dp"), None),
        P(("section", "dp"), None),
        P(("section", "dp")),
        P(("section", "dp")),
    )
    return jax.shard_map(
        shards,
        mesh=mesh,
        in_specs=placed,
        out_specs=(
            P("section", "dp", None),
            P("section", "dp", None),
            P("section", "dp", None),
            P("section", "dp", None),
            P("section", "dp", None),
            P("section", "dp", None),
            P("section", "dp", None),
            P("section", None, "dp"),
            P("section", None, "dp"),
            P(("section", "dp"), None),
            P(("section", "dp"), None),
            P(("section", "dp")),
            P(("section", "dp")),
        ),
        check_vma=False,
    )
```

```python
import math

import jax
import jax.numpy as jnp
from jax import lax
from jax.experimental import pallas as pl
from jax.experimental.pallas import tpu as pltpu
from jax.sharding import PartitionSpec as P

HEAD_DIM = 64
SEQ = 128
NEG_FILL = -1000000000.0
BF = jnp.bfloat16
F32 = jnp.float32


def swap_core(x):
    n = lax.axis_size("dp")
    return lax.ppermute(x, "dp", [(i, i ^ 1) for i in range(n)])


def swap_pair(x):
    n = lax.axis_size("dp")
    return lax.ppermute(x, "dp", [(i, i ^ 2) for i in range(n)])


def spread_outer(x):
    n = lax.axis_size("dp")
    groups = [list(range(at, n, 4)) for at in range(4)]
    x = x.reshape(n // 4, -1, x.shape[1])
    return lax.all_to_all(x, "dp", 0, 0, axis_index_groups=groups)


def shift_outer(x):
    n = lax.axis_size("dp")
    return lax.ppermute(x, "dp", [(i, (i + 4) % n) for i in range(n)])


def gather_by_steps(x):
    pieces = [x]
    for _ in range(lax.axis_size("dp") // 4 - 1):
        pieces.append(shift_outer(pieces[-1]))
    own = jnp.stack(pieces)
    pair = swap_pair(own)
    return jnp.stack([own, pair], axis=1), jnp.stack([to_decoder(own), to_decoder(pair)], axis=1)


def to_decoder(x):
    return lax.ppermute(x, "section", [(0, 1)])


def to_encoder(x):
    return lax.ppermute(x, "section", [(1, 0)])


def after(x, *deps):
    return lax.optimization_barrier((x,) + deps)[0]


def relative_blocks(me, n):
    m = n // 4
    blk = jnp.arange(n)
    crel = 1 - blk // (2 * m)
    xrel = 1 - (blk % (2 * m)) // m
    return (blk % m) * 4 + ((me // 2) % 2 ^ xrel) * 2 + (me % 2 ^ crel)


def order_matrix(order, block, halves=1):
    n = order.shape[0]
    base = order.reshape(2, 1, n // 2, 1) * block
    src = (
        base
        + jnp.arange(halves).reshape(1, halves, 1, 1) * (n * block)
        + jnp.arange(block).reshape(1, 1, 1, block)
    ).reshape(-1)
    return (jnp.arange(src.shape[0])[:, None] == src[None, :]).astype(BF)


def reordered(a, matrix):
    return jnp.einsum("tk,kr->rt", a, matrix, preferred_element_type=F32).astype(BF)


class Chain:
    def __init__(self):
        self.last = ()

    def __call__(self, x):
        return after(x, *self.last) if self.last else x

    def mark(self, *outs):
        self.last = outs
        return outs[0]


def add_low(a, b):
    return (a.astype(F32) + b.astype(F32)).astype(BF)


def summed(blocks):
    return jnp.sum(blocks.astype(F32), axis=0)


class Part:
    def __init__(self, chain, a, dy, got=None, picks=(), columns=None):
        self.chain, self.a, self.dy, self.picks, self.columns = chain, a, dy, picks, columns
        self.k = a.shape[-2]
        self.got = got or [swap_core(piece) for piece in self.outer(0, self.k // 2, pieces=True)]

    def outer(self, first, count, *adds, pieces=False):
        dy = self.chain(self.dy)
        kinds = {"picks": self.picks, "pieces": pieces, "columns": self.columns}
        made = outer(self.a, first, count, dy, *adds, **kinds)
        self.chain.mark(*(made if pieces else (made,)))
        return made

    def pair(self, *deps):
        q, mid = self.k // 4, len(self.got) // 2
        half = self.outer(2 * q, q, (self.got[:mid], 0))
        self.pair_got = swap_pair(after(half, *deps) if deps else half)

    def add(self):
        q, mid = self.k // 4, len(self.got) // 2
        self.mine = self.outer(3 * q, q, (self.got[mid:], 0), ((self.pair_got,), 0))

    def spread(self, *deps):
        self.blocks = spread_outer(after(self.mine, *deps) if deps else self.mine)

    def total(self):
        return summed(self.blocks)


VMEM_LIMIT = 58 * 2**20


def dot(a, b):
    return jnp.dot(a, b, preferred_element_type=F32)


def dot_nt(a, b):
    return lax.dot_general(a, b, (((1,), (1,)), ((), ())), preferred_element_type=F32)


def dot_tn(a, b):
    return lax.dot_general(a, b, (((0,), (0,)), ((), ())), preferred_element_type=F32)


SMEM_SPEC = pl.BlockSpec(memory_space=pltpu.SMEM)
VMEM_SPEC = pl.BlockSpec(memory_space=pltpu.VMEM)
ANY_SPEC = pl.BlockSpec(memory_space=pl.ANY)


def shape_of(rows, columns, dtype=F32):
    return jax.ShapeDtypeStruct((rows, columns), dtype)


def kernel_call(body, out_shape, args, specs, out_specs, name, scratch=(), cost=0):
    return pl.pallas_call(
        body,
        in_specs=specs,
        out_specs=out_specs,
        out_shape=out_shape,
        scratch_shapes=scratch,
        compiler_params=pltpu.CompilerParams(vmem_limit_bytes=VMEM_LIMIT),
        cost_estimate=pl.CostEstimate(flops=cost, bytes_accessed=0, transcendentals=0),
        name=name,
    )(*args)


class Rows:
    def __init__(self, d_loc, inner_width, width):
        self.d = d_loc
        self.width = width
        self.ups = inner_width // width
        self.down_rows = self.ups * d_loc
        self.w_in = 0
        self.qkv = d_loc
        self.attn = 4 * d_loc
        self.up = 5 * d_loc
        self.down = self.up + self.ups * d_loc


def fetch(src, row, rows, dst, sem):
    copy = pltpu.make_async_copy(src.at[:, pl.ds(row, rows)], dst, sem)
    copy.start()
    return copy


def whole(ref):
    value = ref[...]
    return value.reshape(value.shape[0] * value.shape[1], value.shape[2])


def halves(x):
    low_half = lax.broadcasted_iota(jnp.int32, x.shape, 1) < HEAD_DIM
    zero = jnp.zeros_like(x)
    return jnp.where(low_half, x, zero), jnp.where(low_half, zero, x)


def joined(x):
    rows = x.shape[0] // 2
    low_half = lax.broadcasted_iota(jnp.int32, (rows, x.shape[1]), 1) < HEAD_DIM
    return jnp.where(low_half, x[:rows], x[rows:])


def stacked_heads(x):
    return jnp.concatenate(halves(x), axis=0)


def softmax_t(scores, mask):
    logits = jnp.where(mask[None], scores, NEG_FILL)
    e = jnp.exp(logits - jnp.max(logits, axis=1, keepdims=True))
    return e * (1.0 / jnp.sum(e, axis=1, keepdims=True))


FACTOR = HEAD_DIM ** (-0.5)


def probabilities(q, k_stack, mask):
    scores = dot_nt(k_stack, q * jnp.asarray(FACTOR, BF))
    return softmax_t(scores.reshape((2,) + mask.shape), mask)


def attend_lanes(q, k, v, mask):
    probs = probabilities(q, stacked_heads(k), mask).astype(BF)
    return dot_tn(probs.reshape(2 * SEQ, SEQ), stacked_heads(v)).astype(BF)


def attend_back_lanes(g, q, k, v, mask):
    k_stack = stacked_heads(k)
    probs = probabilities(q, k_stack, mask)
    d_probs = dot_nt(stacked_heads(v), g).reshape(probs.shape)
    centred = jnp.sum(probs * d_probs, axis=1, keepdims=True)
    d_s = (probs * (d_probs - centred) * FACTOR).astype(BF).reshape(2 * SEQ, SEQ)
    d_v = joined(dot(probs.astype(BF).reshape(2 * SEQ, SEQ), g))
    d_k = joined(dot(d_s, q))
    return [part.astype(BF) for part in (dot_tn(d_s, k_stack), d_k, d_v)]


def lanes_of(i, offset=0):
    return pl.ds(pl.multiple_of(offset + i * 128, 128), 128)


def attend_all(q_ref, q_at, kv_ref, k_at, v_at, mask_ref, out_ref, width):
    rows = q_ref.shape[0]

    def step(i, carry):
        for b in range(rows // SEQ):
            s = pl.ds(b * SEQ, SEQ)
            out_ref[s, lanes_of(i)] = attend_lanes(
                q_ref[s, lanes_of(i, q_at)],
                kv_ref[s, lanes_of(i, k_at)],
                kv_ref[s, lanes_of(i, v_at)],
                mask_ref[b] > 0,
            )
        return carry

    lax.fori_loop(0, width // 128, step, 0, unroll=4)


def attend_back_all(g_ref, q_ref, q_at, kv_ref, k_at, v_at, mask_ref, out_ref, width):
    rows = g_ref.shape[0]

    def step(i, carry):
        for b in range(rows // SEQ):
            s = pl.ds(b * SEQ, SEQ)
            parts = attend_back_lanes(
                g_ref[s, lanes_of(i)],
                q_ref[s, lanes_of(i, q_at)],
                kv_ref[s, lanes_of(i, k_at)],
                kv_ref[s, lanes_of(i, v_at)],
                mask_ref[b] > 0,
            )
            for at, part in enumerate(parts):
                out_ref[s, lanes_of(i, at * width)] = part
        return carry

    lax.fori_loop(0, width // 128, step, 0, unroll=4)


def norm_values(values, gain, bias):
    centre = values - jnp.mean(values, axis=-1, keepdims=True)
    inverse = lax.rsqrt(jnp.mean(centre * centre, axis=-1, keepdims=True) + 1e-05)
    normed = centre * inverse
    return normed * gain + bias, normed, inverse


def norm_back_values(upstream, normed, inverse, gain):
    scaled = upstream * gain
    return inverse * (
        scaled
        - jnp.mean(scaled, axis=-1, keepdims=True)
        - normed * jnp.mean(scaled * normed, axis=-1, keepdims=True)
    )


def gelu_parts(inner, with_slope):
    erf = 1.0 + lax.erf(inner * (1.0 / math.sqrt(2.0)))
    active = (0.5 * inner * erf).astype(BF)
    if not with_slope:
        return active
    bell = jnp.exp(-0.5 * inner * inner) * (1.0 / math.sqrt(2.0 * math.pi))
    return active, (0.5 * erf + inner * bell).astype(BF)


BLOCK = 512


def column(j, size=BLOCK):
    return pl.ds(pl.multiple_of(j * size, size), size)


def blocks_loop(count, step):
    lax.fori_loop(0, count, lambda j, carry: (step(j), carry)[1], 0, unroll=1 if count % 2 else 2)


def front(tokens, mask, weights, rows_of, gains, biases):
    t = tokens.shape[0]
    n, _, width = weights.shape
    d, ups = rows_of.d, rows_of.ups
    inner_width = ups * width

    def kernel(x_ref, mask_ref, g0, g1, g2, b0, b1, b2, w_hbm, *refs):
        xa_hbm, ia_ref, first_hbm, packed_hbm, mix_hbm, second_hbm, xb_hbm, ib_ref, second_low_hbm, memory_ref = refs[:10]
        w_in, w_qkv, w_attn, w_up, w_down, held, normed, low, packed, mix, second_low, total, active = refs[10:23]
        sems, out_sems = refs[23:]
        first_copy = fetch(w_hbm, rows_of.w_in, d, w_in, sems.at[0])
        qkv_copies = [fetch(w_hbm, rows_of.qkv + i * d, d, w_qkv.at[i], sems.at[1 + i]) for i in range(3)]
        attn_copy = fetch(w_hbm, rows_of.attn, d, w_attn, sems.at[4])
        up_copies = [fetch(w_hbm, rows_of.up + i * d, d, w_up.at[i], sems.at[6 + i]) for i in range(ups)]
        down_copy = fetch(w_hbm, rows_of.down, rows_of.down_rows, w_down, sems.at[5])
        outs = []

        def put(src, dst):
            outs.append(pltpu.make_async_copy(src, dst, out_sems.at[len(outs)]))
            outs[-1].start()

        first_copy.wait()
        first, xa, ia = norm_values(dot(x_ref[...], whole(w_in)), g0[...], b0[...])
        held[...] = first
        normed[...] = xa
        ia_ref[...] = ia
        low[...] = first.astype(BF)
        put(normed, xa_hbm)
        put(low, first_hbm)
        for copy in qkv_copies:
            copy.wait()

        def project(j):
            packed[:, column(j, width)] = dot(
                low[...], w_qkv[j].reshape(n * d, width)
            ).astype(BF)

        blocks_loop(3, project)
        put(packed, packed_hbm)
        attend_all(packed, 0, packed, width, 2 * width, mask_ref, mix, width)
        put(mix, mix_hbm)
        attn_copy.wait()
        second, xb, ib = norm_values(held[...] + dot(mix[...], whole(w_attn)), g1[...], b1[...])
        outs[0].wait()
        held[...] = second
        normed[...] = xb
        ib_ref[...] = ib
        second_low[...] = second.astype(BF)
        put(held, second_hbm)
        put(normed, xb_hbm)
        put(second_low, second_low_hbm)
        for copy in up_copies:
            copy.wait()

        def forward(j):
            active[j] = gelu_parts(dot(second_low[...], w_up[j].reshape(n * d, width)), False)

        blocks_loop(ups, forward)
        down_copy.wait()
        total[...] = second

        def forward_down(j):
            rows = pl.ds(j * (n // ups), n // ups)
            total[...] += dot(active[j], w_down[rows].reshape(width, width))

        blocks_loop(ups, forward_down)
        memory_ref[...] = norm_values(total[...], g2[...], b2[...])[0].astype(BF)
        for copy in outs[1:]:
            copy.wait()

    value, low, vector = shape_of(t, width), shape_of(t, width, BF), shape_of(t, 1)
    big = lambda *shape: pltpu.VMEM(shape, BF)
    return kernel_call(
        kernel,
        (value, vector, low, shape_of(t, 3 * width, BF), low, value, value, vector, low, low),
        (tokens, mask, *gains, *biases, weights),
        [VMEM_SPEC] * 8 + [ANY_SPEC],
        (ANY_SPEC, VMEM_SPEC) + (ANY_SPEC,) * 5 + (VMEM_SPEC, ANY_SPEC, VMEM_SPEC),
        "front",
        scratch=[
            big(n, d, width),
            big(3, n, d, width),
            big(n, d, width),
            big(ups, n, d, width),
            big(n, rows_of.down_rows, width),
            pltpu.VMEM((t, width), F32),
            pltpu.VMEM((t, width), F32),
            big(t, width),
            big(t, 3 * width),
            big(t, width),
            big(t, width),
            pltpu.VMEM((t, width), F32),
            big(ups, t, width),
            pltpu.SemaphoreType.DMA((6 + ups,)),
            pltpu.SemaphoreType.DMA((7,)),
        ],
    )


def arrivals(me, m):
    z, x, core = me // 4, lax.rem(me // 2, 2), lax.rem(me, 2)
    for h in range(2):
        for k in range(m):
            for xrel in range(2):
                outer_pair = lax.rem(z - k + m, m) * 4 + lax.rem(x + xrel, 2) * 2
                yield h, k, xrel, outer_pair + lax.rem(core + h, 2)


class Cross:
    def __init__(self, far, own, me):
        m, _, _, self.c, self.width = own.shape
        self.m, self.n = m, 4 * m
        self.arrays = (far, swap_core(far), own, swap_core(own))
        if self.c % 16:
            index = jnp.stack([j for *_, j in arrivals(me, self.m)])
            back = jnp.sum((index[:, None] == jnp.arange(self.n)) * jnp.arange(self.n)[:, None], axis=0)
            sections = []
            for one, other in (self.arrays[:2], self.arrays[2:]):
                both = jnp.stack([one, other]).reshape(self.n, 4, self.c, self.width)
                sections.append(both[back])
            self.arrays = (jnp.stack(sections).transpose(2, 0, 1, 3, 4),)

    @property
    def specs(self):
        return [ANY_SPEC] * len(self.arrays)

    @property
    def scratch(self):
        return [pltpu.VMEM((4, 2, self.n, self.c, self.width), BF), pltpu.SemaphoreType.DMA((2, 2, self.n))]

    def start(self, refs, dst, sems, me, first, count):
        groups = pl.ds(first, count)
        if len(refs) == 1:
            copies = [pltpu.make_async_copy(refs[0].at[groups], dst.at[groups], sems.at[0, 0])]
        else:
            copies = [
                pltpu.make_async_copy(
                    refs[2 * s + h].at[k, xrel, groups], dst.at[groups, s, j], sems.at[s, i]
                )
                for i, (h, k, xrel, j) in enumerate(arrivals(me, self.m))
                for s in range(2)
            ]
        for copy in copies:
            copy.start()
        return copies

    def matrix(self, ref, i):
        return ref[i].reshape(2 * self.n * self.c, self.width)


def cross_query(info, low, cross):
    t, width = low.shape
    count = len(cross.arrays)

    def kernel(info_ref, low_ref, *refs):
        out_ref, w, sems = refs[count:]
        for copy in cross.start(refs[:count], w, sems.at[0], info_ref[0], 0, 1):
            copy.wait()
        out_ref[...] = dot(low_ref[...], cross.matrix(w, 0)).astype(BF)

    return kernel_call(
        kernel,
        shape_of(t, width, BF),
        (info, low, *cross.arrays),
        [SMEM_SPEC, VMEM_SPEC] + cross.specs,
        VMEM_SPEC,
        "cross_query",
        scratch=cross.scratch,
    )


def cross_query_back(info, resid, d_cross, cross):
    t, width = resid.shape
    count = len(cross.arrays)

    def kernel(info_ref, resid_ref, d_ref, *refs):
        out_ref, w, sems = refs[count:]
        for copy in cross.start(refs[:count], w, sems.at[0], info_ref[0], 0, 1):
            copy.wait()
        out_ref[...] = resid_ref[...] + dot_nt(d_ref[:, :width], cross.matrix(w, 0))

    return kernel_call(
        kernel,
        shape_of(t, width),
        (info, resid, d_cross, *cross.arrays),
        [SMEM_SPEC, VMEM_SPEC, VMEM_SPEC] + cross.specs,
        VMEM_SPEC,
        "cross_query_back",
        scratch=cross.scratch,
    )


def decoder_middle(info, memory, cross_q, second, cot, mask, weights, rows_of, cross, c_gain, c_bias, gain, bias):
    t, width = second.shape
    n, d, ups = weights.shape[0], rows_of.d, rows_of.ups
    inner_width = ups * width
    block = inner_width // n
    ordered = block % 128 == 0
    count = len(cross.arrays)
    per = n // ups

    def kernel(info_ref, memory_ref, q_ref, mask_ref, cg_ref, cb_ref, g_ref, b_ref, second_hbm, cot_hbm, w_hbm, *refs):
        c_refs, refs = refs[:count], refs[count:]
        out_hbm, normed_hbm, inv_ref, third_hbm, active_hbm, slope_hbm = refs[:6]
        mix_ref, d_qkv_ref, d_memory_ref, resid_ref, dg_ref, db_ref = refs[6:12]
        w_c, cross_sems, w_up, w_down, kv, third, low, active, slope, out, normed, c_normed, total, cot = refs[12:26]
        d_branch_ref, sems, act_sems = refs[26:]
        is_dec = info_ref[1] == 1
        copies = cross.start(c_refs, w_c, cross_sems.at[0], info_ref[0], 1, 2)
        get_second = pltpu.make_async_copy(second_hbm, third, sems.at[0])
        get_cot = pltpu.make_async_copy(cot_hbm, cot, sems.at[1])
        get_second.start()
        last_copies = cross.start(c_refs, w_c, cross_sems.at[1], info_ref[0], 3, 1)
        up_copies = [fetch(w_hbm, rows_of.up + i * d, d, w_up.at[i], sems.at[8 + i]) for i in range(ups)]
        down_copy = fetch(w_hbm, rows_of.down, rows_of.down_rows, w_down, sems.at[7])
        get_cot.start()
        for copy in copies:
            copy.wait()
        for i in (1, 2):
            kv[:, (i - 1) * width : i * width] = dot(memory_ref[...], cross.matrix(w_c, i)).astype(BF)
        attend_all(q_ref, 0, kv, 0, width, mask_ref, mix_ref, width)
        get_second.wait()
        for copy in last_copies:
            copy.wait()
        values = third[...] + dot(mix_ref[...], cross.matrix(w_c, 3))
        third_c, normed_c, inverse_c = norm_values(values, cg_ref[...], cb_ref[...])
        c_normed[...] = normed_c
        third[...] = jnp.where(is_dec, third_c, third[...])
        low[...] = third[...].astype(BF)
        outs = [pltpu.make_async_copy(low, third_hbm, sems.at[2])]
        outs[-1].start()
        for copy in up_copies:
            copy.wait()

        def forward(j):
            active[j], slope[j] = gelu_parts(dot(low[...], w_up[j].reshape(n * d, width)), True)

        blocks_loop(ups, forward)
        if not ordered:
            outs.append(pltpu.make_async_copy(active, active_hbm, act_sems.at[0]))
            outs[-1].start()
        for j in range(n if ordered else 0):
            place = info_ref[2 + j]
            outs.append(
                pltpu.make_async_copy(
                    active.at[j // per, :, pl.ds((j % per) * block, block)],
                    active_hbm.at[:, column(place, block)],
                    act_sems.at[j],
                )
            )
            outs[-1].start()
        outs.append(pltpu.make_async_copy(slope, slope_hbm, sems.at[4]))
        outs[-1].start()
        down_copy.wait()
        total[...] = third[...]

        def forward_down(j):
            total[...] += dot(active[j], w_down[pl.ds(j * per, per)].reshape(width, width))

        blocks_loop(ups, forward_down)
        last, normed_d, inverse_d = norm_values(total[...], g_ref[...], b_ref[...])
        out[...] = last
        normed[...] = normed_d
        inv_ref[...] = inverse_d
        outs += [
            pltpu.make_async_copy(out, out_hbm, sems.at[5]),
            pltpu.make_async_copy(normed, normed_hbm, sems.at[6]),
        ]
        outs[-2].start()
        outs[-1].start()
        get_cot.wait()
        grad = norm_back_values(cot[...], normed_d, inverse_d, g_ref[...])
        total[...] = grad
        d_branch_ref[...] = grad.astype(BF)

        def backward(j):
            d_act = dot_nt(d_branch_ref[...], w_down[pl.ds(j * per, per)].reshape(width, width))
            d_inner = (d_act * slope[j].astype(F32)).astype(BF)
            total[...] += dot_nt(d_inner, w_up[j].reshape(n * d, width))

        blocks_loop(ups, backward)
        grad = total[...]
        dg_ref[...] = jnp.sum(grad * c_normed[...], axis=0, keepdims=True)
        db_ref[...] = jnp.sum(grad, axis=0, keepdims=True)
        resid = norm_back_values(grad, c_normed[...], inverse_c, cg_ref[...])
        resid_ref[...] = resid
        d_branch_ref[...] = resid.astype(BF)
        outs[0].wait()
        low[...] = dot_nt(d_branch_ref[...], cross.matrix(w_c, 3)).astype(BF)
        attend_back_all(low, q_ref, 0, kv, 0, width, mask_ref, d_qkv_ref, width)
        d_qkv_ref[:, 3 * width :] = d_branch_ref[...]
        d_memory = dot_nt(d_qkv_ref[:, width : 2 * width], cross.matrix(w_c, 1))
        d_memory_ref[...] = (
            d_memory + dot_nt(d_qkv_ref[:, 2 * width : 3 * width], cross.matrix(w_c, 2))
        ).astype(BF)
        for copy in outs[1:]:
            copy.wait()

    value, low = shape_of(t, width), shape_of(t, width, BF)
    vector, blocked = shape_of(1, width), jax.ShapeDtypeStruct((ups, t, width), BF)
    big = lambda *shape: pltpu.VMEM(shape, BF)
    return kernel_call(
        kernel,
        (value, value, shape_of(t, 1), low)
        + (shape_of(t, inner_width, BF) if ordered else blocked, blocked)
        + (low, shape_of(t, 4 * width, BF), low, value, vector, vector),
        (info, memory, cross_q, mask, c_gain, c_bias, gain, bias, second, cot, weights, *cross.arrays),
        [SMEM_SPEC] + [VMEM_SPEC] * 7 + [ANY_SPEC] * 3 + cross.specs,
        (ANY_SPEC, ANY_SPEC, VMEM_SPEC, ANY_SPEC, ANY_SPEC, ANY_SPEC) + (VMEM_SPEC,) * 6,
        "decoder_middle",
        scratch=cross.scratch
        + [
            big(ups, n, d, width),
            big(n, rows_of.down_rows, width),
            big(t, 2 * width),
            pltpu.VMEM((t, width), F32),
            big(t, width),
            big(ups, t, width),
            big(ups, t, width),
        ]
        + [pltpu.VMEM((t, width), F32)] * 5
        + [
            big(t, width),
            pltpu.SemaphoreType.DMA((8 + ups,)),
            pltpu.SemaphoreType.DMA((n,)),
        ],
    )


def put_pieces(refs, i, count, value):
    rows, size = value.shape
    value = value.astype(BF)
    side, at = divmod(i, count // 2)
    for h in range(2):
        refs[2 * h + side][:, at * size : (at + 1) * size] = value[h * rows // 2 : (h + 1) * rows // 2]


def norm_backward(cot, more, normed, inverse, gain, active_rel):
    t, width = cot.shape
    half = active_rel.shape[0] // 2

    def kernel(cot_ref, more_ref, n_ref, i_ref, gain_ref, a_hbm, *refs):
        grad_ref, low_ref, dg_ref, db_ref, *sent_refs, a, sem = refs
        copy = pltpu.make_async_copy(a_hbm.at[pl.ds(0, half)], a, sem)
        copy.start()
        g = cot_ref[...] + more_ref[...].astype(F32)
        dg_ref[...] = jnp.sum(g * n_ref[...], axis=0, keepdims=True)
        db_ref[...] = jnp.sum(g, axis=0, keepdims=True)
        grad = norm_back_values(g, n_ref[...], i_ref[...], gain_ref[...])
        grad_ref[...] = grad
        low_ref[...] = grad.astype(BF)
        copy.wait()

        for h in range(2):

            def step(j):
                value = dot(a[column(2 * h + j, half // 4)], low_ref[...]).astype(BF)
                for c in range(2):
                    sent_refs[2 * h + c][column(j, half // 4)] = value[:, c * width // 2 : (c + 1) * width // 2]

            blocks_loop(2, step)

    vector = shape_of(1, width)
    return kernel_call(
        kernel,
        (shape_of(t, width), shape_of(t, width, BF), vector, vector)
        + (shape_of(half // 2, width // 2, BF),) * 4,
        (cot, more, normed, inverse, gain, active_rel),
        [VMEM_SPEC] * 5 + [ANY_SPEC],
        (VMEM_SPEC,) * 8,
        "norm_backward",
        scratch=[pltpu.VMEM((half, t), BF), pltpu.SemaphoreType.DMA],
    )


def ffn_backward(branch, slope, weights, rows_of, third_rel):
    t, width = branch.shape
    n, d, ups = weights.shape[0], rows_of.d, rows_of.ups
    per = n // ups
    half = width // 2

    def kernel(branch_ref, slope_ref, a_ref, w_hbm, out_ref, d_inner_ref, *refs):
        *sent_refs, w_up, w_down, sems = refs
        down_copies = [
            pltpu.make_async_copy(
                w_hbm.at[pl.ds(i * per, per), pl.ds(rows_of.down, rows_of.down_rows)],
                w_down.at[pl.ds(i * per, per)],
                sems.at[i],
            )
            for i in range(ups)
        ]
        for copy in down_copies:
            copy.start()
        up_copies = [fetch(w_hbm, rows_of.up + i * d, d, w_up.at[i], sems.at[ups + i]) for i in range(ups)]
        for i in range(ups):
            cols = slice(i * width, (i + 1) * width)
            down_copies[i].wait()
            d_act = dot_nt(branch_ref[...], w_down[i * per : (i + 1) * per].reshape(width, width))
            d_inner_ref[:, cols] = (d_act * slope_ref[i].astype(F32)).astype(BF)
            put_pieces(sent_refs, i, ups, dot(a_ref[:half], d_inner_ref[:, cols]))
        for i in range(ups):
            up_copies[i].wait()
            part = dot_nt(
                d_inner_ref[:, i * width : (i + 1) * width], w_up[i].reshape(n * d, width)
            )
            if i == 0:
                out_ref[...] = part
            else:
                out_ref[...] += part

    return kernel_call(
        kernel,
        (shape_of(t, width), shape_of(t, ups * width, BF)) + (shape_of(half // 2, ups * width // 2, BF),) * 4,
        (branch, slope, third_rel, weights),
        [VMEM_SPEC, VMEM_SPEC, VMEM_SPEC, ANY_SPEC],
        (VMEM_SPEC,) * 6,
        "ffn_backward",
        scratch=[
            pltpu.VMEM((ups, n, d, width), BF),
            pltpu.VMEM((n, rows_of.down_rows, width), BF),
            pltpu.SemaphoreType.DMA((2 * ups,)),
        ],
    )


def attention_backward(info, from_dec, third, inner, normed, inverse, gain, weights, rows_of, packed, mask, stack):
    t, width = third.shape
    n, d = weights.shape[0], rows_of.d
    half = width // 2

    def kernel(info_ref, dec_ref, third_ref, inner_ref, n_ref, i_ref, gain_ref, packed_ref, mask_ref, a_ref, w_hbm, *refs):
        grad_ref, d_ref, dg_ref, db_ref, *sent_refs, w_attn, blended, sem = refs
        copy = fetch(w_hbm, rows_of.attn, d, w_attn, sem)
        g = jnp.where(info_ref[1] == 1, dec_ref[...], third_ref[...] + inner_ref[...])
        dg_ref[...] = jnp.sum(g * n_ref[...], axis=0, keepdims=True)
        db_ref[...] = jnp.sum(g, axis=0, keepdims=True)
        grad = norm_back_values(g, n_ref[...], i_ref[...], gain_ref[...])
        grad_ref[...] = grad
        d_ref[:, 3 * width :] = grad.astype(BF)
        copy.wait()
        blended[...] = dot_nt(d_ref[:, 3 * width :], whole(w_attn)).astype(BF)
        attend_back_all(
            blended, packed_ref, 0, packed_ref, width, 2 * width, mask_ref, d_ref, width
        )
        for i in range(4):
            cols = slice(i * width, (i + 1) * width)
            put_pieces(sent_refs, i, 4, dot(a_ref[0 if i < 3 else 1, :half], d_ref[:, cols]))

    wide, vector = shape_of(t, 4 * width, BF), shape_of(1, width)
    return kernel_call(
        kernel,
        (shape_of(t, width), wide, vector, vector) + (shape_of(half // 2, 2 * width, BF),) * 4,
        (info, from_dec, third, inner, normed, inverse, gain, packed, mask, stack, weights),
        [SMEM_SPEC] + [VMEM_SPEC] * 8 + [VMEM_SPEC, ANY_SPEC],
        (VMEM_SPEC,) * 8,
        "attention_backward",
        scratch=[
            pltpu.VMEM((n, d, width), BF),
            pltpu.VMEM((t, width), BF),
            pltpu.SemaphoreType.DMA,
        ],
    )


def embed_backward(grad, d_packed, normed, inverse, gain, weights, rows_of):
    t, width = grad.shape
    n, d = weights.shape[0], rows_of.d

    def kernel(grad_ref, dp_ref, n_ref, i_ref, gain_ref, w_hbm, *refs):
        low_ref, tokens_ref, dg_ref, db_ref, w_qkv, w_in, total, sems = refs
        copies = [fetch(w_hbm, rows_of.qkv + i * d, d, w_qkv.at[i], sems.at[i]) for i in range(3)]
        last = fetch(w_hbm, rows_of.w_in, d, w_in, sems.at[3])
        total[...] = grad_ref[...]
        for i in range(3):
            copies[i].wait()
            total[...] += dot_nt(
                dp_ref[:, i * width : (i + 1) * width], w_qkv[i].reshape(n * d, width)
            )
        g = total[...]
        dg_ref[...] = jnp.sum(g * n_ref[...], axis=0, keepdims=True)
        db_ref[...] = jnp.sum(g, axis=0, keepdims=True)
        low_ref[...] = norm_back_values(g, n_ref[...], i_ref[...], gain_ref[...]).astype(BF)
        last.wait()
        tokens_ref[...] = dot_nt(low_ref[...], whole(w_in))

    vector = shape_of(1, width)
    return kernel_call(
        kernel,
        (shape_of(t, width, BF), shape_of(t, n * d), vector, vector),
        (grad, d_packed, normed, inverse, gain, weights),
        [VMEM_SPEC, VMEM_SPEC] + [VMEM_SPEC] * 3 + [ANY_SPEC],
        (VMEM_SPEC,) * 4,
        "embed_backward",
        scratch=[
            pltpu.VMEM((3, n, d, width), BF),
            pltpu.VMEM((n, d, width), BF),
            pltpu.VMEM((t, width), F32),
            pltpu.SemaphoreType.DMA((4,)),
        ],
    )


def outer(a, first, count, dy, *adds, picks=(), pieces=False, columns=None):
    t = dy.shape[0]
    start, width = columns or (0, dy.shape[1])
    block = min(width if columns else width // 2, 1024)
    grid = width // block
    mid = grid // 2
    per = grid // max(len(picks), 1)
    stacked = a.ndim == 3
    low = lambda j: jnp.minimum(j, mid - 1)
    high = lambda j: jnp.maximum(j - mid, 0)

    def kernel(a_ref, dy_ref, *refs):
        j = pl.program_id(0)
        value = dot(a_ref[0] if stacked else a_ref[...], dy_ref[...])
        outs = refs[sum(len(parts) for parts, _ in adds) :]
        for parts, _ in adds:
            terms, refs = [ref[...].astype(F32) for ref in refs[: len(parts)]], refs[len(parts) :]
            value = value + (jnp.where(j < mid, *terms) if len(terms) == 2 else terms[0])
        value = value.astype(BF)
        if not pieces:
            outs[0][...] = value
            return

        @pl.when(j < mid)
        def _():
            outs[0][...] = value[: count // 2]
            outs[2][...] = value[count // 2 :]

        @pl.when(j >= mid)
        def _():
            outs[1][...] = value[: count // 2]
            outs[3][...] = value[count // 2 :]

    if stacked:
        pick = lambda j: sum(jnp.where(j // per == i, at, 0) for i, at in enumerate(picks))
        a_spec = pl.BlockSpec((1, count, t), lambda j: (pick(j), first // count, 0))
    else:
        a_spec = pl.BlockSpec((count, t), lambda j: (first // count, 0))
    specs = [a_spec, pl.BlockSpec((t, block), lambda j: (0, start // block + j))]
    for parts, at in adds:
        for place in (low, high) if len(parts) == 2 else (lambda j: j,):
            specs.append(pl.BlockSpec((count, block), lambda j, at=at, place=place: (at // count, place(j))))
    if pieces:
        out_specs = [pl.BlockSpec((count // 2, block), lambda j, place=place: (0, place(j))) for place in (low, high)] * 2
        out_shape = [jax.ShapeDtypeStruct((count // 2, width // 2), BF)] * 4
    else:
        out_specs = pl.BlockSpec((count, block), lambda j: (0, j))
        out_shape = jax.ShapeDtypeStruct((count, width), BF)
    return pl.pallas_call(
        kernel,
        grid=(grid,),
        in_specs=specs,
        out_specs=out_specs,
        out_shape=out_shape,
        compiler_params=pltpu.CompilerParams(vmem_limit_bytes=VMEM_LIMIT),
        cost_estimate=pl.CostEstimate(flops=0, bytes_accessed=0, transcendentals=0),
        name="outer",
    )(a, dy, *[part for parts, _ in adds for part in parts])


def shards(
    section_in,
    segment_ids,
    out_cot,
    in_proj,
    attn_in,
    attn_out,
    ffn_in,
    ffn_out,
    norm_gain,
    norm_bias,
    cross_in,
    cross_out,
    cross_gain,
    cross_bias,
):
    n = lax.axis_size("dp")
    me = lax.axis_index("dp")
    is_dec = lax.axis_index("section") == 1
    width = attn_out.shape[2]
    inner_width = ffn_in.shape[2]
    d_loc = attn_out.shape[1]
    in_loc = in_proj.shape[1]
    c_loc = cross_in.shape[0]
    m = n // 4
    depth = d_loc * n

    order = relative_blocks(me, n)
    places = jnp.sum(jnp.arange(n)[:, None] * (order[:, None] == jnp.arange(n)[None, :]), axis=0)
    info = jnp.concatenate([jnp.stack([me, lax.axis_index("section")]), places]).astype(jnp.int32)

    rows_of = Rows(d_loc, inner_width, width)
    params = jnp.concatenate(
        [norm_gain[0].reshape(-1), norm_bias[0].reshape(-1), cross_gain, cross_bias]
    )
    n_par = params.shape[0]

    def columns_of(w):
        return [w[:, i * width : (i + 1) * width] for i in range(w.shape[1] // width)]

    pack = [in_proj[0], jnp.zeros((d_loc - in_loc, width), F32)]
    pack += columns_of(attn_in[0]) + [attn_out[0]] + columns_of(ffn_in[0]) + [ffn_out[0]]
    weights = lax.all_gather(jnp.concatenate(pack, axis=0).astype(BF), "dp", axis=0)
    own_cross = jnp.stack(columns_of(cross_in) + [cross_out]).astype(BF)
    own_cross, far_cross = gather_by_steps(own_cross)
    cross_w = Cross(far_cross, own_cross, me)

    tokens = section_in[0]
    tokens = tokens.reshape(tokens.shape[0], n, in_loc)
    tokens = jnp.pad(tokens, ((0, 0), (0, 0), (0, d_loc - in_loc))).reshape(-1, depth)
    cot = out_cot[0]
    seqs = tokens.shape[0] // SEQ
    seg = segment_ids.reshape(2, seqs, SEQ)
    own_seg = jnp.where(is_dec, seg[1], seg[0])
    enc_seg = seg[0]
    spots = jnp.arange(SEQ)
    causal = (spots[:, None] <= spots[None, :]) | jnp.logical_not(is_dec)
    self_mask = ((own_seg[:, None, :] == own_seg[:, :, None]) & causal[None]).astype(F32)
    cross_mask = (own_seg[:, None, :] == enc_seg[:, :, None]).astype(F32)
    perm_d = order_matrix(order, d_loc)
    perm_cross = order_matrix(order, c_loc, 2)
    marks = (jnp.arange(depth)[None, :] == (jnp.arange(n) * d_loc + in_loc)[:, None]).astype(BF)
    tokens_rel = reordered(jnp.concatenate([tokens, marks], axis=0), perm_d)

    own_pars, far_pars = gather_by_steps(params.astype(BF)[None])
    pars = jnp.stack([far_pars, own_pars]).reshape(2, n // 2, n_par)
    pars = jnp.concatenate([pars, swap_core(pars)], axis=1)
    index = jnp.stack([j for *_, j in arrivals(me, m)])
    place = (jnp.arange(n)[:, None] == index[None, :]).astype(BF)
    pars = jnp.stack([dot(place, pars[0]), dot(place, pars[1])])

    def vectors(at):
        part = pars[1, :, 3 * at * d_loc : 3 * (at + 1) * d_loc].reshape(n, 3, d_loc)
        part = part.transpose(1, 0, 2).reshape(3, 1, width)
        return [part[i] for i in range(3)]

    gains, biases = vectors(0), vectors(1)
    cpar = pars[:, :, 6 * d_loc :]
    c_gain = cpar[:, :, :c_loc].reshape(1, width)
    c_bias = cpar[:, :, c_loc:].reshape(1, width)

    xa, ia, first_low, packed, blended, second, xb, ib, second_low, encoded = front(
        after(tokens, *cross_w.arrays, c_gain, c_bias, perm_d, perm_cross),
        self_mask,
        weights,
        rows_of,
        gains,
        biases,
    )
    memory = to_decoder(encoded)
    cross_q = cross_query(info, second_low, cross_w)
    attn_rel = jnp.stack([reordered(first_low, perm_d), reordered(blended, perm_d)])
    second_rel = reordered(second_low, perm_cross)
    cross_q = after(cross_q, attn_rel, second_rel, tokens_rel)

    output, xd, idd, third_low, active_rel, slope, cross_mix, d_cross, d_memory, resid, dg_c, db_c = (
        decoder_middle(
            info,
            memory,
            cross_q,
            second,
            cot,
            cross_mask,
            weights,
            rows_of,
            cross_w,
            c_gain,
            c_bias,
            gains[2],
            biases[2],
        )
    )
    grad_memory = to_encoder(d_memory)
    grad_second_dec = cross_query_back(info, resid, d_cross, cross_w)
    third_rel = reordered(third_low, perm_d)
    if active_rel.ndim == 3:
        blocks = active_rel.transpose(1, 0, 2).reshape(tokens.shape[0], n, inner_width // n)
        active_rel = blocks[:, order].reshape(tokens.shape[0], inner_width)
    active_rel = active_rel.T
    cross_rel = jnp.stack(
        [second_rel, reordered(memory, perm_cross), reordered(cross_mix, perm_cross)]
    )
    cvec = jnp.concatenate([dg_c, db_c]).astype(BF).reshape(2, 2, n, c_loc)
    cvec_got = to_encoder(cvec[:, 0])
    cot = after(cot, grad_second_dec, third_rel, cross_rel)

    chain = Chain()
    quarter = width // 4
    grad_d, branch_d, dg_d, db_d, *sent = norm_backward(
        cot, grad_memory, xd, idd, gains[2], active_rel
    )
    chain.mark(*sent)
    got = [swap_core(piece) for piece in sent]
    half = width // 2
    down0 = Part(chain, active_rel, branch_d, got[::2], (), (0, half))
    down1 = Part(chain, active_rel, branch_d, got[1::2], (), (half, half))
    cross = Part(chain, cross_rel, d_cross, picks=(0, 1, 1, 2))
    down0.pair()
    grad_inner, d_inner, *sent = ffn_backward(
        chain(branch_d), slope, weights, rows_of, third_rel
    )
    chain.mark(*sent)
    up = Part(chain, third_rel, d_inner, [swap_core(piece) for piece in sent])
    far = cross.outer(2 * quarter, quarter, (cross.got[:2], 0))
    far = to_encoder(after(far, cvec_got))
    down1.pair(down0.pair_got)
    down0.add()
    down0.spread()
    up.pair()
    grad_b, d_attn, dg_b, db_b, *sent = attention_backward(
        info,
        grad_second_dec,
        grad_d,
        chain(grad_inner),
        xb,
        ib,
        gains[1],
        weights,
        rows_of,
        packed,
        self_mask,
        attn_rel,
    )
    chain.mark(*sent)
    attn = Part(chain, attn_rel, d_attn, [swap_core(piece) for piece in sent], (0, 0, 0, 1))
    down1.add()
    down1.spread(down0.blocks)
    d_embed, d_tokens, dg_a, db_a = embed_backward(
        grad_b, chain(d_attn), xa, ia, gains[0], weights, rows_of
    )
    chain.mark(d_embed)
    cvec = jnp.where(is_dec, cvec[:, 1], cvec_got).transpose(1, 0, 2)
    vecs = jnp.concatenate([dg_a, dg_b, dg_d, db_a, db_b, db_d]).astype(BF)
    vecs = vecs.reshape(6, n, d_loc).transpose(1, 0, 2).reshape(n, 6 * d_loc)
    vecs = jnp.concatenate([vecs, cvec.reshape(n, 2 * c_loc)], axis=1)
    vecs = jnp.pad(vecs, ((0, 0), (0, width - n_par)))
    into = Part(chain, tokens_rel, jnp.concatenate([d_embed, vecs], axis=0))
    near = cross.outer(3 * quarter, quarter, (cross.got[2:], 0))
    near = chain.mark(jnp.where(is_dec, near, far))
    cross_pair = swap_pair(near[: quarter // 2])
    attn.pair()
    into.pair()
    up.add()
    up.spread(down1.blocks)
    cross_total = chain.mark(add_low(near[quarter // 2 :], cross_pair))
    cross_blocks = spread_outer(after(cross_total, up.blocks))
    cross_total = summed(cross_blocks)
    attn.add()
    attn.spread(cross_blocks)
    into.add()
    into.spread(attn.blocks)

    in_grad = chain(d_tokens).reshape(-1, n, d_loc)[:, :, :in_loc].reshape(-1, n * in_loc)
    attn_total = attn.total()
    in_total = into.total()
    row = in_total[in_loc]
    gain_total = row[: 3 * d_loc].reshape(1, 3, d_loc)
    bias_total = row[3 * d_loc : 6 * d_loc].reshape(1, 3, d_loc)

    return (
        output[None],
        in_grad[None],
        in_total[:in_loc][None],
        attn_total[None, :, : 3 * width],
        attn_total[None, :, 3 * width :],
        up.total()[None],
        jnp.concatenate([down0.total(), down1.total()], axis=1)[None],
        gain_total,
        bias_total,
        cross_total[:, : 3 * width],
        cross_total[:, 3 * width :],
        row[6 * d_loc : 6 * d_loc + c_loc],
        row[6 * d_loc + c_loc : n_par],
    )


def solution(mesh):
    placed = (
        P("section", "dp", None),
        P(None, "dp"),
        P("section", "dp", None),
        P("section", "dp", None),
        P("section", "dp", None),
        P("section", "dp", None),
        P("section", "dp", None),
        P("section", "dp", None),
        P("section", None, "dp"),
        P("section", None, "dp"),
        P(("section", "dp"), None),
        P(("section", "dp"), None),
        P(("section", "dp")),
        P(("section", "dp")),
    )
    return jax.shard_map(
        shards,
        mesh=mesh,
        in_specs=placed,
        out_specs=(
            P("section", "dp", None),
            P("section", "dp", None),
            P("section", "dp", None),
            P("section", "dp", None),
            P("section", "dp", None),
            P("section", "dp", None),
            P("section", "dp", None),
            P("section", None, "dp"),
            P("section", None, "dp"),
            P(("section", "dp"), None),
            P(("section", "dp"), None),
            P(("section", "dp")),
            P(("section", "dp")),
        ),
        check_vma=False,
    )
```
